32 devices in a mesh: member: 4 (over y, x), lat: 8 (over z, core).
Axes of the slice: x: 2, y: 2, z: 4, core: 2. Of those that a mesh axis runs over, the one named last changes fastest.
Arguments:
- states: bfloat16 [4, 16, 256, 256], P('member', 'lat'), may hold values from -6 to 6
- member_id: int32 [4], P('member'), may hold values from 0 to 3, each once
- member_gain: float32 [4, 256], replicated, may hold values from 0.5 to 2
- first_conv: bfloat16 [2304, 256], P('member'), may hold values from -0.125 to 0.125
- second_conv: bfloat16 [2304, 256], P('member'), may hold values from -0.125 to 0.125
- head: bfloat16 [256, 8], replicated, may hold values from -0.375 to 0.375
- target: float32 [8, 16, 256], P(None, 'lat'), may hold values from -6 to 6
- lat_start: int32 [1], replicated, may hold values from 0 to 1785
Outputs:
- score: float32 [8, 16, 256], P(None, 'lat')
- mean_score: float32 [], replicated
The draws below stay inside these ranges and needn't reach their ends.
All inputs are finite; a program needn't handle non-finite values.
Results may differ from the reference program's by a relative error of at most 0.0018.
Values may be sent and summed in bfloat16 or wider, within the bound.
A program may use at most 64 MiB of HBM per device.

```python
import math
import jax
import jax.numpy as jnp
from jax import lax

C = 256
K = 8
W = 256
M = 4
ROWS = 16


def levels(stream_key, dims, split, smallest, largest):
    loudness, own = 1.0, jax.random.fold_in(stream_key, 6)
    for dim, parts in split:
        draws = jnp.exp(jax.random.uniform(jax.random.fold_in(own, dim), (parts,), jnp.float32, smallest / len(split), largest / len(split)))
        loudness = loudness * jnp.repeat(draws, dims[dim] // parts).reshape([-1 if axis == dim else 1 for axis in range(len(dims))])
    return loudness


def scatter_about(rng, extent, width, limit, pieces=(), held_as=jnp.bfloat16):
    entries = width * jax.random.normal(rng, extent, jnp.float32)
    if pieces:
        entries = entries * levels(rng, extent, pieces, -0.22, 0.18)
    return jnp.clip(entries, -limit, limit).astype(held_as)


def setup_inputs(seed: int = 0) -> dict:
    key_list = jax.random.split(jax.random.key(seed), 9)
    return {
        "states": scatter_about(key_list[0], (M, ROWS, W, C), 1.0, 6.0, ((0, 4), (1, 8))),
        "member_id": jax.random.permutation(key_list[1], M).astype(jnp.int32),
        "member_gain": jnp.clip(jnp.exp(jax.random.uniform(key_list[2], (M, C), jnp.float32, math.log(0.5), math.log(2.0))), 0.5, 2.0),
        "first_conv": scatter_about(key_list[3], (9 * C, C), (9 * C) ** -0.5, 0.125, ((0, 4),)),
        "second_conv": scatter_about(key_list[4], (9 * C, C), (9 * C) ** -0.5, 0.125, ((0, 4),)),
        "head": scatter_about(key_list[5], (C, K), C ** -0.5, 0.375),
        "target": scatter_about(key_list[6], (K, ROWS, W), 1.0, 6.0, ((1, 8),), jnp.float32),
        "lat_start": jax.random.randint(key_list[7], (1,), 0, 1802 - ROWS).astype(jnp.int32),
    }


def product(left, right):
    return jnp.dot(left.astype(jnp.float32), right.astype(jnp.float32), precision=lax.Precision.HIGHEST, preferred_element_type=jnp.float32)


def convolve(field, weight):
    rows, cols, chans = field.shape
    padded = jnp.pad(field, ((1, 1), (1, 1), (0, 0)))
    taps = [padded[dy:dy + rows, dx:dx + cols, :] for dy in range(3) for dx in range(3)]
    patches = jnp.concatenate(taps, axis=-1).reshape(rows * cols, 9 * chans)
    return product(patches, weight).reshape(rows, cols, -1)


def reference(states, member_id, member_gain, first_conv, second_conv, head, target, lat_start):
    def one_member(args):
        state, ident = args
        select = (jnp.arange(M, dtype=jnp.int32) == ident).astype(jnp.float32)
        gain = jnp.dot(select, member_gain, precision=lax.Precision.HIGHEST)
        start = (state.astype(jnp.float32) * gain).astype(jnp.bfloat16)
        inner = jax.nn.gelu(convolve(start, first_conv), approximate=True).astype(jnp.bfloat16)
        block = (start.astype(jnp.float32) + convolve(inner, second_conv)).astype(jnp.bfloat16)
        pred = product(block.reshape(-1, C), head)
        return pred.T.reshape(K, ROWS, W).astype(jnp.bfloat16)

    preds = lax.map(one_member, (states, member_id)).astype(jnp.float32)
    skill = jnp.sum(jnp.abs(preds - target[None]), axis=0) / M

    def pair_step(total, index):
        return total + jnp.sum(jnp.abs(preds[index][None] - preds), axis=0), None

    spread, _ = lax.scan(pair_step, jnp.zeros((K, ROWS, W), jnp.float32), jnp.arange(M))
    eps = 0.05 / M
    score = skill - (1.0 - eps) / (2.0 * M * (M - 1)) * spread
    rows = lat_start[0].astype(jnp.float32) + jnp.arange(ROWS, dtype=jnp.float32)
    area = jnp.cos(jnp.pi * (90.0 - 0.1 * rows) / 180.0)
    mean_score = jnp.sum(score * area[None, :, None]) / (K * W * jnp.sum(area))
    return score, mean_score
```

```python
import functools
import math

import jax
import jax.numpy as jnp
import numpy as np
from jax import lax
from jax.experimental import pallas as pl
from jax.experimental.pallas import tpu as pltpu
from jax.sharding import PartitionSpec as P

MESH = pl.DeviceIdType.MESH
TAPS = 9


def route(members):
    side = math.isqrt(members)
    return (side, side) if side * side == members else (members, 1)


def legs(i1, i2):
    return (i1 > 0) + (i2 > 0)


def tap_plan(members, chans):
    n1, n2 = route(members)
    shard = TAPS * chans // members
    offsets = sorted(
        ((i1, i2) for i1 in range(n1) for i2 in range(n2)), key=lambda o: legs(*o)
    )
    codes, stages = [], []
    for me in range(members):
        for core in range(2):
            u, v = (1 + core * (n1 - 1), n1 - core * (n1 - 1)) if n2 > 1 else (1, members)
            p1, p2 = (me // u) % n1, (me // v) % n2
            arrival = {}
            for stage, (i1, i2) in enumerate(offsets):
                arrival[((p1 - i1) % n1) * u + ((p2 - i2) % n2) * v] = stage
            need = [
                max(
                    arrival[s]
                    for s in range(t * chans // shard, ((t + 1) * chans - 1) // shard + 1)
                )
                for t in range(TAPS)
            ]
            order = sorted(range(TAPS), key=lambda t: need[t])
            codes.append(sum(t * TAPS**i for i, t in enumerate(order)))
            stages.append([need[t] for t in order])
    return offsets, codes, np.max(np.array(stages), axis=0).tolist()


def kernel(
    members, bands, states, ident, gains, w1, w2, head, target, first_row, score_ref, mean_ref,
    raw, sh, ish, wb1, wb2, acc, acc2, preds, parts,
    local_sem, halo_send, halo_recv, leg_send, leg_recv, sib_send, sib_recv,
    pred_send, pred_recv, part_send, part_recv,
):
    rows, cols, chans = states.shape[1:]
    fields = head.shape[1]
    shard = w1.shape[0]
    n1, n2 = route(members)
    offsets, codes, stage_of = tap_plan(members, chans)
    me = lax.axis_index("member")
    lat = lax.axis_index("lat")
    core = lax.rem(lat, 2)
    sibling = lat + 1 - 2 * core

    barrier = pltpu.get_barrier_semaphore()
    for j in range(1, members):
        pl.semaphore_signal(
            barrier, inc=1, device_id=(lax.rem(me + j, members), lat), device_id_type=MESH
        )
    for j in range(1, bands):
        pl.semaphore_signal(
            barrier, inc=1, device_id=(me, lax.rem(lat + j, bands)), device_id_type=MESH
        )

    own_rows = pl.ds(pl.multiple_of(me * shard, 16), shard)
    locals_ = [
        pltpu.make_async_copy(states.at[0], raw.at[pl.ds(rows, rows)], local_sem.at[0]),
        pltpu.make_async_copy(w1, wb1.at[own_rows], local_sem.at[1]),
        pltpu.make_async_copy(w2, wb2.at[own_rows], local_sem.at[2]),
    ]
    for copy in locals_:
        copy.start()

    lane = lax.broadcasted_iota(jnp.int32, gains.shape, 0)
    gain = jnp.sum(jnp.where(lane == ident[0], gains[...], 0.0), axis=0, keepdims=True)

    def area_of(row):
        return jnp.cos(jnp.pi * (90.0 - 0.1 * row) / 180.0)

    start_row = first_row[0]
    all_rows = rows * bands
    width = -(-all_rows // 128) * 128
    ids = lax.broadcasted_iota(jnp.int32, (8, width), 1)
    area_all = area_of((start_row + ids).astype(jnp.float32))
    area_total = jnp.sum(jnp.where(ids < all_rows, area_all, 0.0)[0:1], axis=1, keepdims=True)
    zeros = jnp.zeros((8, 128), jnp.int32)
    areas = [
        area_of((start_row + lat * rows + r + zeros).astype(jnp.float32))[0:1, 0:1]
        for r in range(rows)
    ]
    head_t = head[...].astype(jnp.float32).T.astype(jnp.bfloat16)

    pl.semaphore_wait(barrier, members - 1 + bands - 1)

    if n2 > 1:
        u, v = 1 + core * (n1 - 1), n1 - core * (n1 - 1)
    else:
        u, v = 1, members
    p1 = lax.rem(me // u, n1)
    p2 = lax.rem(me // v, n2)

    def member_at(q1, q2):
        return q1 * u + q2 * v

    def back(i1, i2):
        return member_at(lax.rem(p1 - i1 + n1, n1), lax.rem(p2 - i2 + n2, n2))

    def half(ref, base, which):
        if shard % 32 == 0:
            return ref.at[pl.ds(pl.multiple_of(base + which * (shard // 2), 16), shard // 2)]
        span = ref.shape[1] // 2
        return ref.at[
            pl.ds(pl.multiple_of(base, 16), shard), pl.ds(pl.multiple_of(which * span, 128), span)
        ]

    def leg_copy(w, i1, i2):
        src, buf = ((w1, wb1), (w2, wb2))[w]
        if i2 == 0:
            dest = member_at(lax.rem(p1 + i1, n1), p2)
            origin, j1 = me, 0
        else:
            dest = member_at(p1, lax.rem(p2 + i2, n2))
            origin, j1 = back(i1, 0), i1
        source = half(src, 0, core) if j1 == 0 else half(buf, origin * shard, core)
        return pltpu.make_async_remote_copy(
            src_ref=source,
            dst_ref=half(buf, origin * shard, core),
            send_sem=leg_send.at[w, i1, i2],
            recv_sem=leg_recv.at[w, i1, i2],
            device_id=(dest, lat),
            device_id_type=MESH,
        )

    def sib_copy(w, i1, i2):
        buf = (wb1, wb2)[w]
        place = half(buf, back(i1, i2) * shard, core)
        return pltpu.make_async_remote_copy(
            src_ref=place,
            dst_ref=place,
            send_sem=sib_send.at[w, i1, i2],
            recv_sem=sib_recv.at[w, i1, i2],
            device_id=(me, sibling),
            device_id_type=MESH,
        )

    def send_own(w):
        for i1 in range(1, n1):
            leg_copy(w, i1, 0).start()
        for i2 in range(1, n2):
            leg_copy(w, 0, i2).start()

    def arrive(w, i1, i2):
        leg_copy(w, i1, i2).wait_recv()
        if i2 == 0:
            for j2 in range(1, n2):
                leg_copy(w, i1, j2).start()
        sib_copy(w, i1, i2).start()

    def halo_copy(step):
        place = pl.ds(0, rows) if step > 0 else pl.ds(2 * rows, rows)
        index = 0 if step > 0 else 1
        return pltpu.make_async_remote_copy(
            src_ref=states.at[0],
            dst_ref=raw.at[place],
            send_sem=halo_send.at[index],
            recv_sem=halo_recv.at[index],
            device_id=(me, lat + step),
            device_id_type=MESH,
        )

    has_low, has_high = lat > 0, lat < bands - 1

    @pl.when(has_high)
    def _():
        halo_copy(1).start()

    @pl.when(has_low)
    def _():
        halo_copy(-1).start()

    send_own(0)

    place_ids = lax.broadcasted_iota(jnp.int32, (cols, chans), 0)

    def put_shifted(ref, row, value):
        low = jnp.where(place_ids == 0, 0.0, pltpu.roll(value, 1, 0))
        high = jnp.where(place_ids == cols - 1, 0.0, pltpu.roll(value, cols - 1, 0))
        ref[0, row] = low.astype(jnp.bfloat16)
        ref[1, row] = value.astype(jnp.bfloat16)
        ref[2, row] = high.astype(jnp.bfloat16)

    def scale_rows(first):
        for r in range(rows):
            value = raw[first + r].astype(jnp.float32) * gain
            put_shifted(sh, first + r, value)

    locals_[0].wait()
    scale_rows(rows)

    @pl.when(has_low)
    def _():
        halo_copy(1).wait_recv()

    @pl.when(jnp.logical_not(has_low))
    def _():
        raw[0:rows] = jnp.zeros((rows, cols, chans), jnp.bfloat16)

    @pl.when(has_high)
    def _():
        halo_copy(-1).wait_recv()

    @pl.when(jnp.logical_not(has_high))
    def _():
        raw[2 * rows : 3 * rows] = jnp.zeros((rows, cols, chans), jnp.bfloat16)

    scale_rows(0)
    scale_rows(2 * rows)

    code = jnp.int32(0)
    combo = me * 2 + core
    for index, value in enumerate(codes):
        code = jnp.where(combo == index, jnp.int32(value), code)

    powers = [TAPS**i for i in range(TAPS)]

    def conv(w, field, total, count, base):
        buf = (wb1, wb2)[w]
        for stage, (i1, i2) in enumerate(offsets):
            if stage == 0:
                locals_[1 + w].wait()
            else:
                if legs(i1, i2) > legs(*offsets[stage - 1]):
                    for o1, o2 in offsets:
                        if legs(o1, o2) == legs(i1, i2) and not (w == 0 and o2 == 0):
                            arrive(w, o1, o2)
                sib_copy(w, *((i2, i1) if n2 > 1 else (i1, i2))).wait_recv()
            mine = [i for i in range(TAPS) if stage_of[i] == stage]
            for i in mine:
                tap = lax.rem(code // powers[i], TAPS)
                dy, dx = tap // 3, lax.rem(tap, 3)
                left = field[dx, pl.ds(base + dy, count)].reshape(count * cols, chans)
                right = buf[pl.ds(pl.multiple_of(tap * chans, 128), chans), :]
                term = jnp.dot(left, right, preferred_element_type=jnp.float32)
                if i == 0:
                    total[...] = term
                else:
                    total[...] += term

    for i1 in range(1, n1):
        arrive(0, i1, 0)
    send_own(1)

    conv(0, sh, acc, rows + 2, rows - 2)

    for r in range(rows + 2):
        value = jax.nn.gelu(acc[pl.ds(r * cols, cols), :], approximate=True)
        if r == 0:
            value = jnp.where(has_low, value, 0.0)
        if r == rows + 1:
            value = jnp.where(has_high, value, 0.0)
        put_shifted(ish, r, value)

    conv(1, ish, acc2, rows, 0)

    own = sh[1, pl.ds(rows, rows)].reshape(rows * cols, chans).astype(jnp.float32)
    block = (own + acc2[...]).astype(jnp.bfloat16)
    pred = lax.dot_general(
        head_t, block, (((1,), (1,)), ((), ())), preferred_element_type=jnp.float32
    )
    pred = jnp.concatenate([pred[:, r * cols : (r + 1) * cols] for r in range(rows)], axis=0)
    preds[me] = pred.astype(jnp.bfloat16)

    pred_copies = [
        pltpu.make_async_remote_copy(
            src_ref=preds.at[me],
            dst_ref=preds.at[me],
            send_sem=pred_send.at[j],
            recv_sem=pred_recv.at[j],
            device_id=(lax.rem(me + j, members), lat),
            device_id_type=MESH,
        )
        for j in range(1, members)
    ]
    for copy in pred_copies:
        copy.start()
    for copy in pred_copies:
        copy.wait_recv()

    eps = 0.05 / members
    factor = (1.0 - eps) / (2.0 * members * (members - 1))
    truth = jnp.concatenate([target[:, r, :] for r in range(rows)], axis=0)
    all_preds = [preds[m].astype(jnp.float32) for m in range(members)]
    skill = sum(jnp.abs(p - truth) for p in all_preds) / members
    pairs = sum(
        jnp.abs(all_preds[m] - all_preds[n]) for m in range(members) for n in range(m)
    )
    score = skill - (2.0 * factor) * pairs
    weighted = jnp.zeros((fields, 128), jnp.float32)
    for r in range(rows):
        piece = score[r * fields : (r + 1) * fields]
        score_ref[:, r, :] = piece
        piece = sum(piece[:, c : c + 128] for c in range(0, cols, 128))
        weighted = weighted + piece * areas[r]
    parts[lat] = weighted

    part_copies = [
        pltpu.make_async_remote_copy(
            src_ref=parts.at[lat],
            dst_ref=parts.at[lat],
            send_sem=part_send.at[j],
            recv_sem=part_recv.at[j],
            device_id=(me, lax.rem(lat + j, bands)),
            device_id_type=MESH,
        )
        for j in range(1, bands)
    ]
    for copy in part_copies:
        copy.start()
    for copy in part_copies:
        copy.wait_recv()
    total = jnp.sum(parts[...], axis=0)
    total = jnp.sum(jnp.sum(total, axis=0, keepdims=True), axis=1, keepdims=True)
    mean = total / (fields * cols * area_total)
    mean_ref[0, 0] = mean[0, 0]

    @pl.when(has_high)
    def _():
        halo_copy(1).wait_send()

    @pl.when(has_low)
    def _():
        halo_copy(-1).wait_send()

    for w in range(2):
        for i1, i2 in offsets[1:]:
            leg_copy(w, i1, i2).wait_send()
            sib_copy(w, i1, i2).wait_send()
    for copy in pred_copies + part_copies:
        copy.wait_send()


def body(members, bands, *args):
    states, head = args[0], args[5]
    rows, cols, chans = states.shape[1:]
    fields = head.shape[1]
    n1, n2 = route(members)
    vmem = pl.BlockSpec(memory_space=pltpu.VMEM)
    smem = pl.BlockSpec(memory_space=pltpu.SMEM)
    anywhere = pl.BlockSpec(memory_space=pl.ANY)
    dma = pltpu.SemaphoreType.DMA
    bf16, f32 = jnp.bfloat16, jnp.float32
    score, mean = pl.pallas_call(
        functools.partial(kernel, members, bands),
        out_shape=(
            jax.ShapeDtypeStruct((fields, rows, cols), f32),
            jax.ShapeDtypeStruct((1, 1), f32),
        ),
        in_specs=[anywhere, smem, vmem, anywhere, anywhere, vmem, vmem, smem],
        out_specs=(vmem, smem),
        scratch_shapes=[
            pltpu.VMEM((3 * rows, cols, chans), bf16),
            pltpu.VMEM((3, 3 * rows, cols, chans), bf16),
            pltpu.VMEM((3, rows + 2, cols, chans), bf16),
            pltpu.VMEM((TAPS * chans, chans), bf16),
            pltpu.VMEM((TAPS * chans, chans), bf16),
            pltpu.VMEM(((rows + 2) * cols, chans), f32),
            pltpu.VMEM((rows * cols, chans), f32),
            pltpu.VMEM((members, rows * fields, cols), bf16),
            pltpu.VMEM((bands, fields, 128), f32),
            dma((3,)),
            dma((2,)),
            dma((2,)),
            dma((2, n1, n2)),
            dma((2, n1, n2)),
            dma((2, n1, n2)),
            dma((2, n1, n2)),
            dma((members,)),
            dma((members,)),
            dma((bands,)),
            dma((bands,)),
        ],
        compiler_params=pltpu.CompilerParams(
            collective_id=0, has_side_effects=True, vmem_limit_bytes=40 * 1024 * 1024
        ),
        cost_estimate=pl.CostEstimate(
            flops=2 * 6 * cols * TAPS * chans * chans,
            bytes_accessed=4 * TAPS * chans * chans,
            transcendentals=4 * cols * chans,
        ),
    )(*args)
    return score, mean[0, 0]


def solution(mesh):
    placed = (
        P("member", "lat", None, None),
        P("member"),
        P(),
        P("member", None),
        P("member", None),
        P(),
        P(None, "lat", None),
        P(),
    )
    return jax.shard_map(
        functools.partial(body, mesh.shape["member"], mesh.shape["lat"]),
        mesh=mesh,
        in_specs=placed,
        out_specs=(P(None, "lat", None), P()),
        check_vma=False,
    )
```

```python
import functools
import math

import jax
import jax.numpy as jnp
import numpy as np
from jax import lax
from jax.experimental import pallas as pl
from jax.experimental.pallas import tpu as pltpu
from jax.sharding import PartitionSpec as P

MESH = pl.DeviceIdType.MESH
TAPS = 9


def route(members):
    side = math.isqrt(members)
    return (side, side) if side * side == members else (members, 1)


def legs(i1, i2):
    return (i1 > 0) + (i2 > 0)


def tap_plan(members, chans):
    n1, n2 = route(members)
    shard = TAPS * chans // members
    offsets = sorted(
        ((i1, i2) for i1 in range(n1) for i2 in range(n2)), key=lambda o: legs(*o)
    )
    codes, stages = [], []
    for me in range(members):
        for core in range(2):
            u, v = (1 + core * (n1 - 1), n1 - core * (n1 - 1)) if n2 > 1 else (1, members)
            p1, p2 = (me // u) % n1, (me // v) % n2
            arrival = {}
            for stage, (i1, i2) in enumerate(offsets):
                arrival[((p1 - i1) % n1) * u + ((p2 - i2) % n2) * v] = stage
            need = [
                max(
                    arrival[s]
                    for s in range(t * chans // shard, ((t + 1) * chans - 1) // shard + 1)
                )
                for t in range(TAPS)
            ]
            order = sorted(range(TAPS), key=lambda t: need[t])
            codes.append(sum(t * TAPS**i for i, t in enumerate(order)))
            stages.append([need[t] for t in order])
    return offsets, codes, np.max(np.array(stages), axis=0).tolist()


def kernel(
    members, bands, states, ident_hbm, gains_hbm, w1, w2, head_hbm, target_hbm, first_row_hbm,
    score_ref, mean_ref, ident, gains, head, target, first_row, raw, sh, ish, wb1, wb2, acc, acc2, preds, parts,
    local_sem, halo_send, halo_recv, leg_send, leg_recv, sib_send, sib_recv,
    pred_send, pred_recv, part_send, part_recv,
):
    rows, cols, chans = states.shape[1:]
    fields = head_hbm.shape[0]
    shard = w1.shape[0]
    n1, n2 = route(members)
    offsets, codes, stage_of = tap_plan(members, chans)
    me = lax.axis_index("member")
    lat = lax.axis_index("lat")
    core = lax.rem(lat, 2)
    sibling = lat + 1 - 2 * core

    barrier = pltpu.get_barrier_semaphore()
    for j in range(1, members):
        pl.semaphore_signal(
            barrier, inc=1, device_id=(lax.rem(me + j, members), lat), device_id_type=MESH
        )
    for j in range(1, bands):
        pl.semaphore_signal(
            barrier, inc=1, device_id=(me, lax.rem(lat + j, bands)), device_id_type=MESH
        )

    own_rows = pl.ds(pl.multiple_of(me * shard, 16), shard)
    locals_ = [
        pltpu.make_async_copy(states.at[0], raw.at[pl.ds(rows, rows)], local_sem.at[0]),
        pltpu.make_async_copy(w1, wb1.at[own_rows], local_sem.at[1]),
        pltpu.make_async_copy(w2, wb2.at[own_rows], local_sem.at[2]),
    ]
    small = [
        pltpu.make_async_copy(source, place, local_sem.at[3 + index])
        for index, (source, place) in enumerate(
            (
                (ident_hbm, ident),
                (gains_hbm, gains),
                (first_row_hbm, first_row),
                (head_hbm, head),
                (target_hbm, target),
            )
        )
    ]
    for copy in small + locals_:
        copy.start()
    for copy in small:
        copy.wait()

    lane = lax.broadcasted_iota(jnp.int32, gains.shape, 0)
    gain = jnp.sum(jnp.where(lane == ident[0], gains[...], 0.0), axis=0, keepdims=True)

    def area_of(row):
        return jnp.cos(jnp.pi * (90.0 - 0.1 * row) / 180.0)

    start_row = first_row[0]
    all_rows = rows * bands
    width = -(-all_rows // 128) * 128
    ids = lax.broadcasted_iota(jnp.int32, (8, width), 1)
    area_all = area_of((start_row + ids).astype(jnp.float32))
    area_total = jnp.sum(jnp.where(ids < all_rows, area_all, 0.0)[0:1], axis=1, keepdims=True)
    zeros = jnp.zeros((8, 128), jnp.int32)
    areas = [
        area_of((start_row + lat * rows + r + zeros).astype(jnp.float32))[0:1, 0:1]
        for r in range(rows)
    ]

    place_ids = lax.broadcasted_iota(jnp.int32, (cols, chans), 0)

    def put_shifted(ref, row, value):
        low = jnp.where(place_ids == 0, 0.0, pltpu.roll(value, 1, 0))
        high = jnp.where(place_ids == cols - 1, 0.0, pltpu.roll(value, cols - 1, 0))
        ref[0, row] = low.astype(jnp.bfloat16)
        ref[1, row] = value.astype(jnp.bfloat16)
        ref[2, row] = high.astype(jnp.bfloat16)

    def scale_rows(first):
        for r in range(rows):
            value = raw[first + r].astype(jnp.float32) * gain
            put_shifted(sh, first + r, value)

    locals_[0].wait()
    scale_rows(rows)

    pl.semaphore_wait(barrier, members - 1 + bands - 1)

    if n2 > 1:
        u, v = 1 + core * (n1 - 1), n1 - core * (n1 - 1)
    else:
        u, v = 1, members
    p1 = lax.rem(me // u, n1)
    p2 = lax.rem(me // v, n2)

    def member_at(q1, q2):
        return q1 * u + q2 * v

    def back(i1, i2):
        return member_at(lax.rem(p1 - i1 + n1, n1), lax.rem(p2 - i2 + n2, n2))

    def half(ref, base, which):
        if shard % 32 == 0:
            return ref.at[pl.ds(pl.multiple_of(base + which * (shard // 2), 16), shard // 2)]
        span = ref.shape[1] // 2
        return ref.at[
            pl.ds(pl.multiple_of(base, 16), shard), pl.ds(pl.multiple_of(which * span, 128), span)
        ]

    def leg_copy(w, i1, i2):
        src, buf = ((w1, wb1), (w2, wb2))[w]
        if i2 == 0:
            dest = member_at(lax.rem(p1 + i1, n1), p2)
            origin, j1 = me, 0
        else:
            dest = member_at(p1, lax.rem(p2 + i2, n2))
            origin, j1 = back(i1, 0), i1
        source = half(src, 0, core) if j1 == 0 else half(buf, origin * shard, core)
        return pltpu.make_async_remote_copy(
            src_ref=source,
            dst_ref=half(buf, origin * shard, core),
            send_sem=leg_send.at[w, i1, i2],
            recv_sem=leg_recv.at[w, i1, i2],
            device_id=(dest, lat),
            device_id_type=MESH,
        )

    def sib_copy(w, i1, i2):
        buf = (wb1, wb2)[w]
        place = half(buf, back(i1, i2) * shard, core)
        return pltpu.make_async_remote_copy(
            src_ref=place,
            dst_ref=place,
            send_sem=sib_send.at[w, i1, i2],
            recv_sem=sib_recv.at[w, i1, i2],
            device_id=(me, sibling),
            device_id_type=MESH,
        )

    def send_own(w):
        for i1 in range(1, n1):
            leg_copy(w, i1, 0).start()
        for i2 in range(1, n2):
            leg_copy(w, 0, i2).start()

    def arrive(w, i1, i2):
        leg_copy(w, i1, i2).wait_recv()
        if i2 == 0:
            for j2 in range(1, n2):
                leg_copy(w, i1, j2).start()
        sib_copy(w, i1, i2).start()

    def halo_copy(step):
        place = pl.ds(0, rows) if step > 0 else pl.ds(2 * rows, rows)
        index = 0 if step > 0 else 1
        return pltpu.make_async_remote_copy(
            src_ref=states.at[0],
            dst_ref=raw.at[place],
            send_sem=halo_send.at[index],
            recv_sem=halo_recv.at[index],
            device_id=(me, lat + step),
            device_id_type=MESH,
        )

    send_own(0)
    has_low, has_high = lat > 0, lat < bands - 1

    @pl.when(has_high)
    def _():
        halo_copy(1).start()

    @pl.when(has_low)
    def _():
        halo_copy(-1).start()

    for i1 in range(1, n1):
        arrive(0, i1, 0)
    send_own(1)


    @pl.when(has_low)
    def _():
        halo_copy(1).wait_recv()

    @pl.when(jnp.logical_not(has_low))
    def _():
        raw[0:rows] = jnp.zeros((rows, cols, chans), jnp.bfloat16)

    @pl.when(has_high)
    def _():
        halo_copy(-1).wait_recv()

    @pl.when(jnp.logical_not(has_high))
    def _():
        raw[2 * rows : 3 * rows] = jnp.zeros((rows, cols, chans), jnp.bfloat16)

    scale_rows(0)
    scale_rows(2 * rows)

    code = jnp.int32(0)
    combo = me * 2 + core
    for index, value in enumerate(codes):
        code = jnp.where(combo == index, jnp.int32(value), code)

    powers = [TAPS**i for i in range(TAPS)]

    def conv(w, field, total, count, base):
        buf = (wb1, wb2)[w]
        for stage, (i1, i2) in enumerate(offsets):
            if stage == 0:
                locals_[1 + w].wait()
            else:
                if legs(i1, i2) > legs(*offsets[stage - 1]):
                    for o1, o2 in offsets:
                        if legs(o1, o2) == legs(i1, i2) and not (w == 0 and o2 == 0):
                            arrive(w, o1, o2)
                sib_copy(w, *((i2, i1) if n2 > 1 else (i1, i2))).wait_recv()
            mine = [i for i in range(TAPS) if stage_of[i] == stage]
            for i in mine:
                tap = lax.rem(code // powers[i], TAPS)
                dy, dx = tap // 3, lax.rem(tap, 3)
                left = field[dx, pl.ds(base + dy, count)].reshape(count * cols, chans)
                right = buf[pl.ds(pl.multiple_of(tap * chans, 128), chans), :]
                term = jnp.dot(left, right, preferred_element_type=jnp.float32)
                if i == 0:
                    total[...] = term
                else:
                    total[...] += term

    conv(0, sh, acc, rows + 2, rows - 2)

    for r in range(rows + 2):
        value = jax.nn.gelu(acc[pl.ds(r * cols, cols), :], approximate=True)
        if r == 0:
            value = jnp.where(has_low, value, 0.0)
        if r == rows + 1:
            value = jnp.where(has_high, value, 0.0)
        put_shifted(ish, r, value)

    conv(1, ish, acc2, rows, 0)

    own = sh[1, pl.ds(rows, rows)].reshape(rows * cols, chans).astype(jnp.float32)
    block = (own + acc2[...]).astype(jnp.bfloat16)
    pred = lax.dot_general(
        head[...], block, (((1,), (1,)), ((), ())), preferred_element_type=jnp.float32
    )
    pred = jnp.concatenate([pred[:, r * cols : (r + 1) * cols] for r in range(rows)], axis=0)
    preds[me] = pred.astype(jnp.bfloat16)

    pred_copies = [
        pltpu.make_async_remote_copy(
            src_ref=preds.at[me],
            dst_ref=preds.at[me],
            send_sem=pred_send.at[j],
            recv_sem=pred_recv.at[j],
            device_id=(lax.rem(me + j, members), lat),
            device_id_type=MESH,
        )
        for j in range(1, members)
    ]
    for copy in pred_copies:
        copy.start()
    for copy in pred_copies:
        copy.wait_recv()

    eps = 0.05 / members
    factor = (1.0 - eps) / (2.0 * members * (members - 1))
    truth = jnp.concatenate([target[:, r, :] for r in range(rows)], axis=0)
    all_preds = [preds[m].astype(jnp.float32) for m in range(members)]
    skill = sum(jnp.abs(p - truth) for p in all_preds) / members
    pairs = sum(
        jnp.abs(all_preds[m] - all_preds[n]) for m in range(members) for n in range(m)
    )
    score = skill - (2.0 * factor) * pairs
    weighted = jnp.zeros((fields, 128), jnp.float32)
    for r in range(rows):
        piece = score[r * fields : (r + 1) * fields]
        score_ref[:, r, :] = piece
        piece = sum(piece[:, c : c + 128] for c in range(0, cols, 128))
        weighted = weighted + piece * areas[r]
    parts[lat] = weighted

    part_copies = [
        pltpu.make_async_remote_copy(
            src_ref=parts.at[lat],
            dst_ref=parts.at[lat],
            send_sem=part_send.at[j],
            recv_sem=part_recv.at[j],
            device_id=(me, lax.rem(lat + j, bands)),
            device_id_type=MESH,
        )
        for j in range(1, bands)
    ]
    for copy in part_copies:
        copy.start()
    for copy in part_copies:
        copy.wait_recv()
    total = jnp.sum(parts[...], axis=0)
    total = jnp.sum(jnp.sum(total, axis=0, keepdims=True), axis=1, keepdims=True)
    mean = total / (fields * cols * area_total)
    mean_ref[0, 0] = mean[0, 0]

    @pl.when(has_high)
    def _():
        halo_copy(1).wait_send()

    @pl.when(has_low)
    def _():
        halo_copy(-1).wait_send()

    for w in range(2):
        for i1, i2 in offsets[1:]:
            leg_copy(w, i1, i2).wait_send()
            sib_copy(w, i1, i2).wait_send()
    for copy in pred_copies + part_copies:
        copy.wait_send()


def body(members, bands, *args):
    states, head = args[0], args[5]
    rows, cols, chans = states.shape[1:]
    fields = head.shape[1]
    args = args[:5] + (head.T,) + args[6:]
    n1, n2 = route(members)
    hbm = pl.BlockSpec(memory_space=pltpu.HBM)
    vmem = pl.BlockSpec(memory_space=pltpu.VMEM)
    smem = pl.BlockSpec(memory_space=pltpu.SMEM)
    dma = pltpu.SemaphoreType.DMA
    bf16, f32 = jnp.bfloat16, jnp.float32
    score, mean = pl.pallas_call(
        functools.partial(kernel, members, bands),
        out_shape=(
            jax.ShapeDtypeStruct((fields, rows, cols), f32),
            jax.ShapeDtypeStruct((1, 1), f32),
        ),
        in_specs=[hbm] * 8,
        out_specs=(vmem, smem),
        scratch_shapes=[
            pltpu.SMEM((1,), jnp.int32),
            pltpu.VMEM(args[2].shape, f32),
            pltpu.VMEM((fields, chans), bf16),
            pltpu.VMEM(args[6].shape, f32),
            pltpu.SMEM((1,), jnp.int32),
            pltpu.VMEM((3 * rows, cols, chans), bf16),
            pltpu.VMEM((3, 3 * rows, cols, chans), bf16),
            pltpu.VMEM((3, rows + 2, cols, chans), bf16),
            pltpu.VMEM((TAPS * chans, chans), bf16),
            pltpu.VMEM((TAPS * chans, chans), bf16),
            pltpu.VMEM(((rows + 2) * cols, chans), f32),
            pltpu.VMEM((rows * cols, chans), f32),
            pltpu.VMEM((members, rows * fields, cols), bf16),
            pltpu.VMEM((bands, fields, 128), f32),
            dma((8,)),
            dma((2,)),
            dma((2,)),
            dma((2, n1, n2)),
            dma((2, n1, n2)),
            dma((2, n1, n2)),
            dma((2, n1, n2)),
            dma((members,)),
            dma((members,)),
            dma((bands,)),
            dma((bands,)),
        ],
        compiler_params=pltpu.CompilerParams(
            collective_id=0, has_side_effects=True, vmem_limit_bytes=62 * 1024 * 1024
        ),
        cost_estimate=pl.CostEstimate(
            flops=2 * 6 * cols * TAPS * chans * chans,
            bytes_accessed=4 * TAPS * chans * chans,
            transcendentals=4 * cols * chans,
        ),
    )(*args)
    return score, mean[0, 0]


def solution(mesh):
    placed = (
        P("member", "lat", None, None),
        P("member"),
        P(),
        P("member", None),
        P("member", None),
        P(),
        P(None, "lat", None),
        P(),
    )
    return jax.shard_map(
        functools.partial(body, mesh.shape["member"], mesh.shape["lat"]),
        mesh=mesh,
        in_specs=placed,
        out_specs=(P(None, "lat", None), P()),
        check_vma=False,
    )
```

```python
import functools
import math

import jax
import jax.numpy as jnp
import numpy as np
from jax import lax
from jax.experimental import pallas as pl
from jax.experimental.pallas import tpu as pltpu
from jax.sharding import PartitionSpec as P

MESH = pl.DeviceIdType.MESH
TAPS = 9


def route(members):
    side = math.isqrt(members)
    return (side, side) if side * side == members else (members, 1)


def legs(i1, i2):
    return (i1 > 0) + (i2 > 0)


def tap_plan(members, chans):
    n1, n2 = route(members)
    shard = TAPS * chans // members
    offsets = sorted(
        ((i1, i2) for i1 in range(n1) for i2 in range(n2)), key=lambda o: legs(*o)
    )
    codes, stages = [], []
    for me in range(members):
        for core in range(2):
            u, v = (1 + core * (n1 - 1), n1 - core * (n1 - 1)) if n2 > 1 else (1, members)
            p1, p2 = (me // u) % n1, (me // v) % n2
            arrival = {}
            for stage, (i1, i2) in enumerate(offsets):
                arrival[((p1 - i1) % n1) * u + ((p2 - i2) % n2) * v] = stage
            need = [
                max(
                    arrival[s]
                    for s in range(t * chans // shard, ((t + 1) * chans - 1) // shard + 1)
                )
                for t in range(TAPS)
            ]
            order = sorted(range(TAPS), key=lambda t: need[t])
            codes.append(sum(t * TAPS**i for i, t in enumerate(order)))
            stages.append([need[t] for t in order])
    return offsets, codes, np.max(np.array(stages), axis=0).tolist()


def chunk_count(shard):
    return 2 if shard % 64 == 0 else 1


def kernel(
    members, bands, states, ident_hbm, gains_hbm, w1, w2, head_hbm, target_hbm, first_row_hbm,
    score_ref, mean_ref, ident, gains, head, target, first_row, raw, sh, ish, wb1, wb2, acc, acc2, preds, parts,
    local_sem, halo_send, halo_recv, leg_send, leg_recv, sib_send, sib_recv,
    pred_send, pred_recv, part_send, part_recv,
):
    rows, cols, chans = states.shape[1:]
    fields = head_hbm.shape[0]
    shard = w1.shape[0]
    n1, n2 = route(members)
    offsets, codes, stage_of = tap_plan(members, chans)
    me = lax.axis_index("member")
    lat = lax.axis_index("lat")
    core = lax.rem(lat, 2)
    sibling = lat + 1 - 2 * core

    barrier = pltpu.get_barrier_semaphore()
    for j in range(1, members):
        pl.semaphore_signal(
            barrier, inc=1, device_id=(lax.rem(me + j, members), lat), device_id_type=MESH
        )
    for j in range(1, bands):
        pl.semaphore_signal(
            barrier, inc=1, device_id=(me, lax.rem(lat + j, bands)), device_id_type=MESH
        )

    own_rows = pl.ds(pl.multiple_of(me * shard, 16), shard)
    locals_ = [
        pltpu.make_async_copy(states.at[0], raw.at[pl.ds(rows, rows)], local_sem.at[0]),
        pltpu.make_async_copy(w1, wb1.at[own_rows], local_sem.at[1]),
        pltpu.make_async_copy(w2, wb2.at[own_rows], local_sem.at[2]),
    ]
    small = [
        pltpu.make_async_copy(source, place, local_sem.at[3 + index])
        for index, (source, place) in enumerate(
            (
                (ident_hbm, ident),
                (gains_hbm, gains),
                (first_row_hbm, first_row),
                (head_hbm, head),
                (target_hbm, target),
            )
        )
    ]
    for copy in small + locals_:
        copy.start()
    for copy in small:
        copy.wait()

    lane = lax.broadcasted_iota(jnp.int32, gains.shape, 0)
    gain = jnp.sum(jnp.where(lane == ident[0], gains[...], 0.0), axis=0, keepdims=True)

    def area_of(row):
        return jnp.cos(jnp.pi * (90.0 - 0.1 * row) / 180.0)

    start_row = first_row[0]
    all_rows = rows * bands
    width = -(-all_rows // 128) * 128
    ids = lax.broadcasted_iota(jnp.int32, (8, width), 1)
    area_all = area_of((start_row + ids).astype(jnp.float32))
    area_total = jnp.sum(jnp.where(ids < all_rows, area_all, 0.0)[0:1], axis=1, keepdims=True)
    zeros = jnp.zeros((8, 128), jnp.int32)
    areas = [
        area_of((start_row + lat * rows + r + zeros).astype(jnp.float32))[0:1, 0:1]
        for r in range(rows)
    ]

    place_ids = lax.broadcasted_iota(jnp.int32, (cols, chans), 0)

    def put_shifted(ref, row, value):
        low = jnp.where(place_ids == 0, 0.0, pltpu.roll(value, 1, 0))
        high = jnp.where(place_ids == cols - 1, 0.0, pltpu.roll(value, cols - 1, 0))
        ref[0, row] = low.astype(jnp.bfloat16)
        ref[1, row] = value.astype(jnp.bfloat16)
        ref[2, row] = high.astype(jnp.bfloat16)

    def scale_rows(first):
        for r in range(rows):
            value = raw[first + r].astype(jnp.float32) * gain
            put_shifted(sh, first + r, value)

    locals_[0].wait()
    scale_rows(rows)

    pl.semaphore_wait(barrier, members - 1 + bands - 1)

    if n2 > 1:
        u, v = 1 + core * (n1 - 1), n1 - core * (n1 - 1)
    else:
        u, v = 1, members
    p1 = lax.rem(me // u, n1)
    p2 = lax.rem(me // v, n2)

    def member_at(q1, q2):
        return q1 * u + q2 * v

    def back(i1, i2):
        return member_at(lax.rem(p1 - i1 + n1, n1), lax.rem(p2 - i2 + n2, n2))

    chunks = chunk_count(shard)

    def half(ref, base, which, chunk):
        if shard % (32 * chunks) == 0:
            size = shard // (2 * chunks)
            first = base + which * (shard // 2) + chunk * size
            return ref.at[pl.ds(pl.multiple_of(first, 16), size)]
        span = ref.shape[1] // 2
        return ref.at[
            pl.ds(pl.multiple_of(base, 16), shard), pl.ds(pl.multiple_of(which * span, 128), span)
        ]

    def leg_copy(w, i1, i2, chunk):
        src, buf = ((w1, wb1), (w2, wb2))[w]
        if i2 == 0:
            dest = member_at(lax.rem(p1 + i1, n1), p2)
            origin, j1 = me, 0
        else:
            dest = member_at(p1, lax.rem(p2 + i2, n2))
            origin, j1 = back(i1, 0), i1
        source = (
            half(src, 0, core, chunk) if j1 == 0 else half(buf, origin * shard, core, chunk)
        )
        return pltpu.make_async_remote_copy(
            src_ref=source,
            dst_ref=half(buf, origin * shard, core, chunk),
            send_sem=leg_send.at[w, i1, i2, chunk],
            recv_sem=leg_recv.at[w, i1, i2, chunk],
            device_id=(dest, lat),
            device_id_type=MESH,
        )

    def sib_copy(w, i1, i2, chunk):
        buf = (wb1, wb2)[w]
        place = half(buf, back(i1, i2) * shard, core, chunk)
        return pltpu.make_async_remote_copy(
            src_ref=place,
            dst_ref=place,
            send_sem=sib_send.at[w, i1, i2, chunk],
            recv_sem=sib_recv.at[w, i1, i2, chunk],
            device_id=(me, sibling),
            device_id_type=MESH,
        )

    def send_own(w):
        for chunk in range(chunks):
            for i1 in range(1, n1):
                leg_copy(w, i1, 0, chunk).start()
            for i2 in range(1, n2):
                leg_copy(w, 0, i2, chunk).start()

    def arrive(w, i1, i2):
        for chunk in range(chunks):
            leg_copy(w, i1, i2, chunk).wait_recv()
            if i2 == 0:
                for j2 in range(1, n2):
                    leg_copy(w, i1, j2, chunk).start()
            sib_copy(w, i1, i2, chunk).start()

    def halo_copy(step):
        place = pl.ds(0, rows) if step > 0 else pl.ds(2 * rows, rows)
        index = 0 if step > 0 else 1
        return pltpu.make_async_remote_copy(
            src_ref=states.at[0],
            dst_ref=raw.at[place],
            send_sem=halo_send.at[index],
            recv_sem=halo_recv.at[index],
            device_id=(me, lat + step),
            device_id_type=MESH,
        )

    send_own(0)
    has_low, has_high = lat > 0, lat < bands - 1

    @pl.when(has_high)
    def _():
        halo_copy(1).start()

    @pl.when(has_low)
    def _():
        halo_copy(-1).start()

    for i1 in range(1, n1):
        arrive(0, i1, 0)
    send_own(1)


    @pl.when(has_low)
    def _():
        halo_copy(1).wait_recv()

    @pl.when(jnp.logical_not(has_low))
    def _():
        raw[0:rows] = jnp.zeros((rows, cols, chans), jnp.bfloat16)

    @pl.when(has_high)
    def _():
        halo_copy(-1).wait_recv()

    @pl.when(jnp.logical_not(has_high))
    def _():
        raw[2 * rows : 3 * rows] = jnp.zeros((rows, cols, chans), jnp.bfloat16)

    scale_rows(0)
    scale_rows(2 * rows)

    code = jnp.int32(0)
    combo = me * 2 + core
    for index, value in enumerate(codes):
        code = jnp.where(combo == index, jnp.int32(value), code)

    powers = [TAPS**i for i in range(TAPS)]

    def conv(w, field, total, count, base):
        buf = (wb1, wb2)[w]
        for stage, (i1, i2) in enumerate(offsets):
            if stage == 0:
                locals_[1 + w].wait()
            else:
                if legs(i1, i2) > legs(*offsets[stage - 1]):
                    for o1, o2 in offsets:
                        if legs(o1, o2) == legs(i1, i2) and o2 > 0:
                            arrive(w, o1, o2)
                for chunk in range(chunks):
                    sib_copy(w, *((i2, i1) if n2 > 1 else (i1, i2)), chunk).wait_recv()
            mine = [i for i in range(TAPS) if stage_of[i] == stage]
            for i in mine:
                tap = lax.rem(code // powers[i], TAPS)
                dy, dx = tap // 3, lax.rem(tap, 3)
                left = field[dx, pl.ds(base + dy, count)].reshape(count * cols, chans)
                right = buf[pl.ds(pl.multiple_of(tap * chans, 128), chans), :]
                term = jnp.dot(left, right, preferred_element_type=jnp.float32)
                if i == 0:
                    total[...] = term
                else:
                    total[...] += term

    conv(0, sh, acc, rows + 2, rows - 2)

    for i1 in range(1, n1):
        arrive(1, i1, 0)

    for r in range(rows + 2):
        value = jax.nn.gelu(acc[pl.ds(r * cols, cols), :], approximate=True)
        if r == 0:
            value = jnp.where(has_low, value, 0.0)
        if r == rows + 1:
            value = jnp.where(has_high, value, 0.0)
        put_shifted(ish, r, value)

    conv(1, ish, acc2, rows, 0)

    own = sh[1, pl.ds(rows, rows)].reshape(rows * cols, chans).astype(jnp.float32)
    block = (own + acc2[...]).astype(jnp.bfloat16)
    pred = lax.dot_general(
        head[...], block, (((1,), (1,)), ((), ())), preferred_element_type=jnp.float32
    )
    pred = jnp.concatenate([pred[:, r * cols : (r + 1) * cols] for r in range(rows)], axis=0)
    preds[me] = pred.astype(jnp.bfloat16)

    pred_copies = [
        pltpu.make_async_remote_copy(
            src_ref=preds.at[me],
            dst_ref=preds.at[me],
            send_sem=pred_send.at[j],
            recv_sem=pred_recv.at[j],
            device_id=(lax.rem(me + j, members), lat),
            device_id_type=MESH,
        )
        for j in range(1, members)
    ]
    for copy in pred_copies:
        copy.start()
    for copy in pred_copies:
        copy.wait_recv()

    eps = 0.05 / members
    factor = (1.0 - eps) / (2.0 * members * (members - 1))
    truth = jnp.concatenate([target[:, r, :] for r in range(rows)], axis=0)
    all_preds = [preds[m].astype(jnp.float32) for m in range(members)]
    skill = sum(jnp.abs(p - truth) for p in all_preds) / members
    pairs = sum(
        jnp.abs(all_preds[m] - all_preds[n]) for m in range(members) for n in range(m)
    )
    score = skill - (2.0 * factor) * pairs
    weighted = jnp.zeros((fields, 128), jnp.float32)
    for r in range(rows):
        piece = score[r * fields : (r + 1) * fields]
        score_ref[:, r, :] = piece
        piece = sum(piece[:, c : c + 128] for c in range(0, cols, 128))
        weighted = weighted + piece * areas[r]
    parts[lat] = weighted

    part_copies = [
        pltpu.make_async_remote_copy(
            src_ref=parts.at[lat],
            dst_ref=parts.at[lat],
            send_sem=part_send.at[j],
            recv_sem=part_recv.at[j],
            device_id=(me, lax.rem(lat + j, bands)),
            device_id_type=MESH,
        )
        for j in range(1, bands)
    ]
    for copy in part_copies:
        copy.start()
    for copy in part_copies:
        copy.wait_recv()
    total = jnp.sum(parts[...], axis=0)
    total = jnp.sum(jnp.sum(total, axis=0, keepdims=True), axis=1, keepdims=True)
    mean = total / (fields * cols * area_total)
    mean_ref[0, 0] = mean[0, 0]

    @pl.when(has_high)
    def _():
        halo_copy(1).wait_send()

    @pl.when(has_low)
    def _():
        halo_copy(-1).wait_send()

    for w in range(2):
        for i1, i2 in offsets[1:]:
            for chunk in range(chunks):
                leg_copy(w, i1, i2, chunk).wait_send()
                sib_copy(w, i1, i2, chunk).wait_send()
    for copy in pred_copies + part_copies:
        copy.wait_send()


def body(members, bands, *args):
    states, head = args[0], args[5]
    rows, cols, chans = states.shape[1:]
    fields = head.shape[1]
    args = args[:5] + (head.T,) + args[6:]
    n1, n2 = route(members)
    chunks = chunk_count(args[3].shape[0])
    hbm = pl.BlockSpec(memory_space=pltpu.HBM)
    vmem = pl.BlockSpec(memory_space=pltpu.VMEM)
    smem = pl.BlockSpec(memory_space=pltpu.SMEM)
    dma = pltpu.SemaphoreType.DMA
    bf16, f32 = jnp.bfloat16, jnp.float32
    score, mean = pl.pallas_call(
        functools.partial(kernel, members, bands),
        out_shape=(
            jax.ShapeDtypeStruct((fields, rows, cols), f32),
            jax.ShapeDtypeStruct((1, 1), f32),
        ),
        in_specs=[hbm] * 8,
        out_specs=(vmem, smem),
        scratch_shapes=[
            pltpu.SMEM((1,), jnp.int32),
            pltpu.VMEM(args[2].shape, f32),
            pltpu.VMEM((fields, chans), bf16),
            pltpu.VMEM(args[6].shape, f32),
            pltpu.SMEM((1,), jnp.int32),
            pltpu.VMEM((3 * rows, cols, chans), bf16),
            pltpu.VMEM((3, 3 * rows, cols, chans), bf16),
            pltpu.VMEM((3, rows + 2, cols, chans), bf16),
            pltpu.VMEM((TAPS * chans, chans), bf16),
            pltpu.VMEM((TAPS * chans, chans), bf16),
            pltpu.VMEM(((rows + 2) * cols, chans), f32),
            pltpu.VMEM((rows * cols, chans), f32),
            pltpu.VMEM((members, rows * fields, cols), bf16),
            pltpu.VMEM((bands, fields, 128), f32),
            dma((8,)),
            dma((2,)),
            dma((2,)),
            dma((2, n1, n2, chunks)),
            dma((2, n1, n2, chunks)),
            dma((2, n1, n2, chunks)),
            dma((2, n1, n2, chunks)),
            dma((members,)),
            dma((members,)),
            dma((bands,)),
            dma((bands,)),
        ],
        compiler_params=pltpu.CompilerParams(
            collective_id=0, has_side_effects=True, vmem_limit_bytes=62 * 1024 * 1024
        ),
        cost_estimate=pl.CostEstimate(
            flops=2 * 6 * cols * TAPS * chans * chans,
            bytes_accessed=4 * TAPS * chans * chans,
            transcendentals=4 * cols * chans,
        ),
    )(*args)
    return score, mean[0, 0]


def solution(mesh):
    placed = (
        P("member", "lat", None, None),
        P("member"),
        P(),
        P("member", None),
        P("member", None),
        P(),
        P(None, "lat", None),
        P(),
    )
    return jax.shard_map(
        functools.partial(body, mesh.shape["member"], mesh.shape["lat"]),
        mesh=mesh,
        in_specs=placed,
        out_specs=(P(None, "lat", None), P()),
        check_vma=False,
    )
```

```python
import functools
import math

import jax
import jax.numpy as jnp
import numpy as np
from jax import lax
from jax.experimental import pallas as pl
from jax.experimental.pallas import tpu as pltpu
from jax.sharding import PartitionSpec as P

MESH = pl.DeviceIdType.MESH
TAPS = 9


def route(members):
    side = math.isqrt(members)
    return (side, side) if side * side == members else (members, 1)


def legs(i1, i2):
    return (i1 > 0) + (i2 > 0)


def tap_plan(members, chans):
    n1, n2 = route(members)
    shard = TAPS * chans // members
    offsets = sorted(
        ((i1, i2) for i1 in range(n1) for i2 in range(n2)), key=lambda o: legs(*o)
    )
    codes, stages = [], []
    for me in range(members):
        for core in range(2):
            u, v = (1 + core * (n1 - 1), n1 - core * (n1 - 1)) if n2 > 1 else (1, members)
            p1, p2 = (me // u) % n1, (me // v) % n2
            arrival = {}
            for stage, (i1, i2) in enumerate(offsets):
                arrival[((p1 - i1) % n1) * u + ((p2 - i2) % n2) * v] = stage
            need = [
                max(
                    arrival[s]
                    for s in range(t * chans // shard, ((t + 1) * chans - 1) // shard + 1)
                )
                for t in range(TAPS)
            ]
            order = sorted(range(TAPS), key=lambda t: need[t])
            codes.append(sum(t * TAPS**i for i, t in enumerate(order)))
            stages.append([need[t] for t in order])
    return offsets, codes, np.max(np.array(stages), axis=0).tolist()


def chunk_count(shard):
    return 2 if shard % 64 == 0 else 1


def kernel(
    members, bands, states, ident_hbm, gains_hbm, w1, w2, head_hbm, target_hbm, first_row_hbm,
    score_ref, mean_ref, ident, gains, head, target, first_row, gain_ref, raw, sh, ish, wb1, wb2, acc, acc2, preds, parts,
    local_sem, halo_send, halo_recv, leg_send, leg_recv, sib_send, sib_recv,
    pred_send, pred_recv, part_send, part_recv,
):
    rows, cols, chans = states.shape[1:]
    fields = head_hbm.shape[0]
    shard = w1.shape[0]
    n1, n2 = route(members)
    offsets, codes, stage_of = tap_plan(members, chans)
    me = lax.axis_index("member")
    lat = lax.axis_index("lat")
    core = lax.rem(lat, 2)
    sibling = lat + 1 - 2 * core

    barrier = pltpu.get_barrier_semaphore()
    for j in range(1, members):
        pl.semaphore_signal(
            barrier, inc=1, device_id=(lax.rem(me + j, members), lat), device_id_type=MESH
        )
    for j in range(1, bands):
        pl.semaphore_signal(
            barrier, inc=1, device_id=(me, lax.rem(lat + j, bands)), device_id_type=MESH
        )

    own_rows = pl.ds(pl.multiple_of(me * shard, 16), shard)
    locals_ = [
        pltpu.make_async_copy(states.at[0], raw.at[pl.ds(rows, rows)], local_sem.at[0]),
        pltpu.make_async_copy(w1, wb1.at[own_rows], local_sem.at[1]),
        pltpu.make_async_copy(w2, wb2.at[own_rows], local_sem.at[2]),
    ]
    small = [
        pltpu.make_async_copy(source, place, local_sem.at[3 + index])
        for index, (source, place) in enumerate(
            (
                (ident_hbm, ident),
                (gains_hbm, gains),
                (first_row_hbm, first_row),
                (head_hbm, head),
                (target_hbm, target),
            )
        )
    ]
    for copy in small + locals_:
        copy.start()
    for copy in small:
        copy.wait()

    lane = lax.broadcasted_iota(jnp.int32, gains.shape, 0)
    gain = jnp.sum(jnp.where(lane == ident[0], gains[...], 0.0), axis=0, keepdims=True)

    all_rows = rows * bands
    width = -(-all_rows // 128) * 128
    ids = lax.broadcasted_iota(jnp.int32, (8, width), 1)
    area_all = jnp.cos(jnp.pi * (90.0 - 0.1 * (first_row[0] + ids).astype(jnp.float32)) / 180.0)

    def area_sum(chosen):
        return jnp.sum(jnp.where(chosen, area_all, 0.0)[0:1], axis=1, keepdims=True)

    area_total = area_sum(ids < all_rows)
    areas = [area_sum(ids == lat * rows + r) for r in range(rows)]

    strip = 128
    strips = chans // strip
    place_ids = lax.broadcasted_iota(jnp.int32, (cols, strip), 0)

    def lanes_of(index):
        return pl.ds(pl.multiple_of(lax.rem(index, strips) * strip, strip), strip)

    def put_shifted(ref, row, lanes, value):
        low = jnp.where(place_ids == 0, 0.0, pltpu.roll(value, 1, 0))
        high = jnp.where(place_ids == cols - 1, 0.0, pltpu.roll(value, cols - 1, 0))
        ref[0, row, :, lanes] = low.astype(jnp.bfloat16)
        ref[1, row, :, lanes] = value.astype(jnp.bfloat16)
        ref[2, row, :, lanes] = high.astype(jnp.bfloat16)

    def scale_rows(count, place):
        @pl.loop(0, count * strips)
        def _(index):
            row, lanes = place(index // strips), lanes_of(index)
            value = raw[row, :, lanes].astype(jnp.float32) * gain_ref[0:1, lanes]
            put_shifted(sh, row, lanes, value)

    gain_ref[...] = jnp.broadcast_to(gain, gain_ref.shape)
    locals_[0].wait()
    scale_rows(rows, lambda r: r + rows)
    acc[...] = jnp.zeros_like(acc)
    acc2[...] = jnp.zeros_like(acc2)

    pl.semaphore_wait(barrier, members - 1 + bands - 1)

    if n2 > 1:
        u, v = 1 + core * (n1 - 1), n1 - core * (n1 - 1)
    else:
        u, v = 1, members
    p1 = lax.rem(me // u, n1)
    p2 = lax.rem(me // v, n2)

    def member_at(q1, q2):
        return q1 * u + q2 * v

    def back(i1, i2):
        return member_at(lax.rem(p1 - i1 + n1, n1), lax.rem(p2 - i2 + n2, n2))

    chunks = chunk_count(shard)

    def half(ref, base, which, chunk):
        if shard % (32 * chunks) == 0:
            size = shard // (2 * chunks)
            first = base + which * (shard // 2) + chunk * size
            return ref.at[pl.ds(pl.multiple_of(first, 16), size)]
        span = ref.shape[1] // 2
        return ref.at[
            pl.ds(pl.multiple_of(base, 16), shard), pl.ds(pl.multiple_of(which * span, 128), span)
        ]

    def leg_copy(w, i1, i2, chunk):
        src, buf = ((w1, wb1), (w2, wb2))[w]
        if i2 == 0:
            dest = member_at(lax.rem(p1 + i1, n1), p2)
            origin, j1 = me, 0
        else:
            dest = member_at(p1, lax.rem(p2 + i2, n2))
            origin, j1 = back(i1, 0), i1
        source = (
            half(src, 0, core, chunk) if j1 == 0 else half(buf, origin * shard, core, chunk)
        )
        return pltpu.make_async_remote_copy(
            src_ref=source,
            dst_ref=half(buf, origin * shard, core, chunk),
            send_sem=leg_send.at[w, i1, i2, chunk],
            recv_sem=leg_recv.at[w, i1, i2, chunk],
            device_id=(dest, lat),
            device_id_type=MESH,
        )

    def sib_copy(w, i1, i2, chunk):
        buf = (wb1, wb2)[w]
        place = half(buf, back(i1, i2) * shard, core, chunk)
        return pltpu.make_async_remote_copy(
            src_ref=place,
            dst_ref=place,
            send_sem=sib_send.at[w, i1, i2, chunk],
            recv_sem=sib_recv.at[w, i1, i2, chunk],
            device_id=(me, sibling),
            device_id_type=MESH,
        )

    def send_own(w):
        for chunk in range(chunks):
            for i1 in range(1, n1):
                leg_copy(w, i1, 0, chunk).start()
            for i2 in range(1, n2):
                leg_copy(w, 0, i2, chunk).start()

    def arrive(w, i1, i2):
        for chunk in range(chunks):
            leg_copy(w, i1, i2, chunk).wait_recv()
            if i2 == 0:
                for j2 in range(1, n2):
                    leg_copy(w, i1, j2, chunk).start()
            sib_copy(w, i1, i2, chunk).start()

    def halo_copy(step):
        place = pl.ds(0, rows) if step > 0 else pl.ds(2 * rows, rows)
        index = 0 if step > 0 else 1
        return pltpu.make_async_remote_copy(
            src_ref=states.at[0],
            dst_ref=raw.at[place],
            send_sem=halo_send.at[index],
            recv_sem=halo_recv.at[index],
            device_id=(me, lat + step),
            device_id_type=MESH,
        )

    send_own(0)
    has_low, has_high = lat > 0, lat < bands - 1

    @pl.when(has_high)
    def _():
        halo_copy(1).start()

    @pl.when(has_low)
    def _():
        halo_copy(-1).start()

    for i1 in range(1, n1):
        arrive(0, i1, 0)
    send_own(1)


    @pl.when(has_low)
    def _():
        halo_copy(1).wait_recv()

    @pl.when(jnp.logical_not(has_low))
    def _():
        raw[0:rows] = jnp.zeros((rows, cols, chans), jnp.bfloat16)

    @pl.when(has_high)
    def _():
        halo_copy(-1).wait_recv()

    @pl.when(jnp.logical_not(has_high))
    def _():
        raw[2 * rows : 3 * rows] = jnp.zeros((rows, cols, chans), jnp.bfloat16)

    scale_rows(2 * rows, lambda r: r + rows * (r // rows))

    code = jnp.int32(0)
    combo = me * 2 + core
    for index, value in enumerate(codes):
        code = jnp.where(combo == index, jnp.int32(value), code)

    def stage_waits(w, stage):
        i1, i2 = offsets[stage]
        if stage == 0:
            locals_[1 + w].wait()
            return
        if legs(i1, i2) > legs(*offsets[stage - 1]):
            for o1, o2 in offsets:
                if legs(o1, o2) == legs(i1, i2) and o2 > 0:
                    arrive(w, o1, o2)
        for chunk in range(chunks):
            sib_copy(w, *((i2, i1) if n2 > 1 else (i1, i2)), chunk).wait_recv()

    def conv(w, field, total, count, base):
        buf = (wb1, wb2)[w]

        def step(i, left_code):
            done = 0
            for at in range(TAPS):
                due = list(range(done, stage_of[at] + 1))
                done = max(done, stage_of[at] + 1)
                if due:

                    @pl.when(i == at)
                    def _():
                        for stage in due:
                            stage_waits(w, stage)

            tap = lax.rem(left_code, TAPS)
            dy, dx = tap // 3, lax.rem(tap, 3)
            left = field[dx, pl.ds(base + dy, count)].reshape(count * cols, chans)
            right = buf[pl.ds(pl.multiple_of(tap * chans, 128), chans), :]
            total[...] += jnp.dot(left, right, preferred_element_type=jnp.float32)
            return left_code // TAPS

        lax.fori_loop(0, TAPS, step, code)

    conv(0, sh, acc, rows + 2, rows - 2)

    for i1 in range(1, n1):
        arrive(1, i1, 0)

    @pl.loop(0, (rows + 2) * strips)
    def _(index):
        row, lanes = index // strips, lanes_of(index)
        at = pl.ds(pl.multiple_of(row * cols, cols), cols)
        value = jax.nn.gelu(acc[at, lanes], approximate=True)
        inside = jnp.logical_and(
            jnp.logical_or(row > 0, has_low), jnp.logical_or(row < rows + 1, has_high)
        )
        put_shifted(ish, row, lanes, jnp.where(inside, value, 0.0))

    conv(1, ish, acc2, rows, 0)

    own = sh[1, pl.ds(rows, rows)].reshape(rows * cols, chans).astype(jnp.float32)
    block = (own + acc2[...]).astype(jnp.bfloat16)
    pred = lax.dot_general(
        head[...], block, (((1,), (1,)), ((), ())), preferred_element_type=jnp.float32
    )
    pred = jnp.concatenate([pred[:, r * cols : (r + 1) * cols] for r in range(rows)], axis=0)
    preds[me] = pred.astype(jnp.bfloat16)

    pred_copies = [
        pltpu.make_async_remote_copy(
            src_ref=preds.at[me],
            dst_ref=preds.at[me],
            send_sem=pred_send.at[j],
            recv_sem=pred_recv.at[j],
            device_id=(lax.rem(me + j, members), lat),
            device_id_type=MESH,
        )
        for j in range(1, members)
    ]
    for copy in pred_copies:
        copy.start()
    for copy in pred_copies:
        copy.wait_recv()

    eps = 0.05 / members
    factor = (1.0 - eps) / (2.0 * members * (members - 1))
    truth = jnp.concatenate([target[:, r, :] for r in range(rows)], axis=0)
    all_preds = [preds[m].astype(jnp.float32) for m in range(members)]
    skill = sum(jnp.abs(p - truth) for p in all_preds) / members
    pairs = sum(
        jnp.abs(all_preds[m] - all_preds[n]) for m in range(members) for n in range(m)
    )
    score = skill - (2.0 * factor) * pairs
    weighted = jnp.zeros((fields, 128), jnp.float32)
    for r in range(rows):
        piece = score[r * fields : (r + 1) * fields]
        score_ref[:, r, :] = piece
        piece = sum(piece[:, c : c + 128] for c in range(0, cols, 128))
        weighted = weighted + piece * areas[r]
    parts[lat] = weighted

    part_copies = [
        pltpu.make_async_remote_copy(
            src_ref=parts.at[lat],
            dst_ref=parts.at[lat],
            send_sem=part_send.at[j],
            recv_sem=part_recv.at[j],
            device_id=(me, lax.rem(lat + j, bands)),
            device_id_type=MESH,
        )
        for j in range(1, bands)
    ]
    for copy in part_copies:
        copy.start()
    for copy in part_copies:
        copy.wait_recv()
    total = jnp.sum(parts[...], axis=0)
    total = jnp.sum(jnp.sum(total, axis=0, keepdims=True), axis=1, keepdims=True)
    mean = total / (fields * cols * area_total)
    mean_ref[0, 0] = mean[0, 0]

    @pl.when(has_high)
    def _():
        halo_copy(1).wait_send()

    @pl.when(has_low)
    def _():
        halo_copy(-1).wait_send()

    for w in range(2):
        for i1, i2 in offsets[1:]:
            for chunk in range(chunks):
                leg_copy(w, i1, i2, chunk).wait_send()
                sib_copy(w, i1, i2, chunk).wait_send()
    for copy in pred_copies + part_copies:
        copy.wait_send()


def body(members, bands, *args):
    states, head = args[0], args[5]
    rows, cols, chans = states.shape[1:]
    fields = head.shape[1]
    args = args[:5] + (head.T,) + args[6:]
    n1, n2 = route(members)
    chunks = chunk_count(args[3].shape[0])
    hbm = pl.BlockSpec(memory_space=pltpu.HBM)
    vmem = pl.BlockSpec(memory_space=pltpu.VMEM)
    smem = pl.BlockSpec(memory_space=pltpu.SMEM)
    dma = pltpu.SemaphoreType.DMA
    bf16, f32 = jnp.bfloat16, jnp.float32
    score, mean = pl.pallas_call(
        functools.partial(kernel, members, bands),
        out_shape=(
            jax.ShapeDtypeStruct((fields, rows, cols), f32),
            jax.ShapeDtypeStruct((1, 1), f32),
        ),
        in_specs=[hbm] * 8,
        out_specs=(vmem, smem),
        scratch_shapes=[
            pltpu.SMEM((1,), jnp.int32),
            pltpu.VMEM(args[2].shape, f32),
            pltpu.VMEM((fields, chans), bf16),
            pltpu.VMEM(args[6].shape, f32),
            pltpu.SMEM((1,), jnp.int32),
            pltpu.VMEM((8, chans), f32),
            pltpu.VMEM((3 * rows, cols, chans), bf16),
            pltpu.VMEM((3, 3 * rows, cols, chans), bf16),
            pltpu.VMEM((3, rows + 2, cols, chans), bf16),
            pltpu.VMEM((TAPS * chans, chans), bf16),
            pltpu.VMEM((TAPS * chans, chans), bf16),
            pltpu.VMEM(((rows + 2) * cols, chans), f32),
            pltpu.VMEM((rows * cols, chans), f32),
            pltpu.VMEM((members, rows * fields, cols), bf16),
            pltpu.VMEM((bands, fields, 128), f32),
            dma((8,)),
            dma((2,)),
            dma((2,)),
            dma((2, n1, n2, chunks)),
            dma((2, n1, n2, chunks)),
            dma((2, n1, n2, chunks)),
            dma((2, n1, n2, chunks)),
            dma((members,)),
            dma((members,)),
            dma((bands,)),
            dma((bands,)),
        ],
        compiler_params=pltpu.CompilerParams(
            collective_id=0, has_side_effects=True, vmem_limit_bytes=62 * 1024 * 1024
        ),
        cost_estimate=pl.CostEstimate(
            flops=2 * 6 * cols * TAPS * chans * chans,
            bytes_accessed=4 * TAPS * chans * chans,
            transcendentals=4 * cols * chans,
        ),
    )(*args)
    return score, mean[0, 0]


def solution(mesh):
    placed = (
        P("member", "lat", None, None),
        P("member"),
        P(),
        P("member", None),
        P("member", None),
        P(),
        P(None, "lat", None),
        P(),
    )
    return jax.shard_map(
        functools.partial(body, mesh.shape["member"], mesh.shape["lat"]),
        mesh=mesh,
        in_specs=placed,
        out_specs=(P(None, "lat", None), P()),
        check_vma=False,
    )
```

```python
import functools
import math

import jax
import jax.numpy as jnp
import numpy as np
from jax import lax
from jax.experimental import pallas as pl
from jax.experimental.pallas import tpu as pltpu
from jax.sharding import PartitionSpec as P

MESH = pl.DeviceIdType.MESH
TAPS = 9


def route(members):
    side = math.isqrt(members)
    return (side, side) if side * side == members else (members, 1)


def legs(i1, i2):
    return (i1 > 0) + (i2 > 0)


def tap_plan(members, chans):
    n1, n2 = route(members)
    shard = TAPS * chans // members
    offsets = sorted(
        ((i1, i2) for i1 in range(n1) for i2 in range(n2)), key=lambda o: legs(*o)
    )
    codes, stages = [], []
    for me in range(members):
        for core in range(2):
            u, v = (1 + core * (n1 - 1), n1 - core * (n1 - 1)) if n2 > 1 else (1, members)
            p1, p2 = (me // u) % n1, (me // v) % n2
            arrival = {}
            for stage, (i1, i2) in enumerate(offsets):
                arrival[((p1 - i1) % n1) * u + ((p2 - i2) % n2) * v] = stage
            need = [
                max(
                    arrival[s]
                    for s in range(t * chans // shard, ((t + 1) * chans - 1) // shard + 1)
                )
                for t in range(TAPS)
            ]
            order = sorted(range(TAPS), key=lambda t: need[t])
            codes.append(sum(t * TAPS**i for i, t in enumerate(order)))
            stages.append([need[t] for t in order])
    return offsets, codes, np.max(np.array(stages), axis=0).tolist()


def chunk_count(shard):
    return 2 if shard % 64 == 0 else 1


def kernel(
    members, bands, states, ident_hbm, gains_hbm, w1, w2, head_hbm, target_hbm, first_row_hbm,
    score_ref, mean_ref, ident, gains, head, target, first_row, gain_ref, raw, sh, ish, wb1, wb2, acc, acc2, preds, parts,
    local_sem, halo_send, halo_recv, leg_send, leg_recv, sib_send, sib_recv,
    pred_send, pred_recv, part_send, part_recv,
):
    rows, cols, chans = states.shape[1:]
    fields = head_hbm.shape[0]
    shard = w1.shape[0]
    n1, n2 = route(members)
    offsets, codes, stage_of = tap_plan(members, chans)
    me = lax.axis_index("member")
    lat = lax.axis_index("lat")
    core = lax.rem(lat, 2)
    sibling = lat + 1 - 2 * core

    barrier = pltpu.get_barrier_semaphore()
    for j in range(1, members):
        pl.semaphore_signal(
            barrier, inc=1, device_id=(lax.rem(me + j, members), lat), device_id_type=MESH
        )
    for j in range(1, bands):
        pl.semaphore_signal(
            barrier, inc=1, device_id=(me, lax.rem(lat + j, bands)), device_id_type=MESH
        )

    own_rows = pl.ds(pl.multiple_of(me * shard, 16), shard)
    locals_ = [
        pltpu.make_async_copy(states.at[0], raw.at[pl.ds(rows, rows)], local_sem.at[0]),
        pltpu.make_async_copy(w1, wb1.at[own_rows], local_sem.at[1]),
        pltpu.make_async_copy(w2, wb2.at[own_rows], local_sem.at[2]),
    ]
    small = [
        pltpu.make_async_copy(source, place, local_sem.at[3 + index])
        for index, (source, place) in enumerate(
            (
                (ident_hbm, ident),
                (gains_hbm, gains),
                (first_row_hbm, first_row),
                (head_hbm, head),
                (target_hbm, target),
            )
        )
    ]
    for copy in small + locals_:
        copy.start()
    for copy in small:
        copy.wait()

    lane = lax.broadcasted_iota(jnp.int32, gains.shape, 0)
    gain = jnp.sum(jnp.where(lane == ident[0], gains[...], 0.0), axis=0, keepdims=True)

    all_rows = rows * bands
    width = -(-all_rows // 128) * 128
    ids = lax.broadcasted_iota(jnp.int32, (8, width), 1)
    area_all = jnp.cos(jnp.pi * (90.0 - 0.1 * (first_row[0] + ids).astype(jnp.float32)) / 180.0)

    def area_sum(chosen):
        return jnp.sum(jnp.where(chosen, area_all, 0.0)[0:1], axis=1, keepdims=True)

    area_total = area_sum(ids < all_rows)
    areas = [area_sum(ids == lat * rows + r) for r in range(rows)]

    strip = 128
    strips = chans // strip
    place_ids = lax.broadcasted_iota(jnp.int32, (cols, strip), 0)

    def lanes_of(index):
        return pl.ds(pl.multiple_of(lax.rem(index, strips) * strip, strip), strip)

    def put_shifted(ref, row, lanes, value):
        low = jnp.where(place_ids == 0, 0.0, pltpu.roll(value, 1, 0))
        high = jnp.where(place_ids == cols - 1, 0.0, pltpu.roll(value, cols - 1, 0))
        ref[0, row, :, lanes] = low.astype(jnp.bfloat16)
        ref[1, row, :, lanes] = value.astype(jnp.bfloat16)
        ref[2, row, :, lanes] = high.astype(jnp.bfloat16)

    def scale_rows(count, place):
        @pl.loop(0, count * strips)
        def _(index):
            row, lanes = place(index // strips), lanes_of(index)
            value = raw[row, :, lanes].astype(jnp.float32) * gain_ref[0:1, lanes]
            put_shifted(sh, row, lanes, value)

    gain_ref[...] = jnp.broadcast_to(gain, gain_ref.shape)
    locals_[0].wait()
    scale_rows(rows, lambda r: r + rows)
    acc[...] = jnp.zeros_like(acc)
    acc2[...] = jnp.zeros_like(acc2)

    pl.semaphore_wait(barrier, members - 1 + bands - 1)

    if n2 > 1:
        u, v = 1 + core * (n1 - 1), n1 - core * (n1 - 1)
    else:
        u, v = 1, members
    p1 = lax.rem(me // u, n1)
    p2 = lax.rem(me // v, n2)

    def member_at(q1, q2):
        return q1 * u + q2 * v

    def back(i1, i2):
        return member_at(lax.rem(p1 - i1 + n1, n1), lax.rem(p2 - i2 + n2, n2))

    chunks = chunk_count(shard)

    def half(ref, base, which, chunk):
        if shard % (32 * chunks) == 0:
            size = shard // (2 * chunks)
            first = base + which * (shard // 2) + chunk * size
            return ref.at[pl.ds(pl.multiple_of(first, 16), size)]
        span = ref.shape[1] // 2
        return ref.at[
            pl.ds(pl.multiple_of(base, 16), shard), pl.ds(pl.multiple_of(which * span, 128), span)
        ]

    def leg_copy(w, i1, i2, chunk):
        src, buf = ((w1, wb1), (w2, wb2))[w]
        if i2 == 0:
            dest = member_at(lax.rem(p1 + i1, n1), p2)
            origin, j1 = me, 0
        else:
            dest = member_at(p1, lax.rem(p2 + i2, n2))
            origin, j1 = back(i1, 0), i1
        source = (
            half(src, 0, core, chunk) if j1 == 0 else half(buf, origin * shard, core, chunk)
        )
        return pltpu.make_async_remote_copy(
            src_ref=source,
            dst_ref=half(buf, origin * shard, core, chunk),
            send_sem=leg_send.at[w, i1, i2, chunk],
            recv_sem=leg_recv.at[w, i1, i2, chunk],
            device_id=(dest, lat),
            device_id_type=MESH,
        )

    def sib_copy(w, i1, i2, chunk):
        buf = (wb1, wb2)[w]
        place = half(buf, back(i1, i2) * shard, core, chunk)
        return pltpu.make_async_remote_copy(
            src_ref=place,
            dst_ref=place,
            send_sem=sib_send.at[w, i1, i2, chunk],
            recv_sem=sib_recv.at[w, i1, i2, chunk],
            device_id=(me, sibling),
            device_id_type=MESH,
        )

    def send_own(w, some):
        for chunk in some:
            for i1 in range(1, n1):
                leg_copy(w, i1, 0, chunk).start()
            for i2 in range(1, n2):
                leg_copy(w, 0, i2, chunk).start()

    def arrive(w, i1, i2, some=range(chunks)):
        for chunk in some:
            leg_copy(w, i1, i2, chunk).wait_recv()
            if i2 == 0:
                for j2 in range(1, n2):
                    leg_copy(w, i1, j2, chunk).start()
            sib_copy(w, i1, i2, chunk).start()

    def halo_copy(step):
        place = pl.ds(0, rows) if step > 0 else pl.ds(2 * rows, rows)
        index = 0 if step > 0 else 1
        return pltpu.make_async_remote_copy(
            src_ref=states.at[0],
            dst_ref=raw.at[place],
            send_sem=halo_send.at[index],
            recv_sem=halo_recv.at[index],
            device_id=(me, lat + step),
            device_id_type=MESH,
        )

    send_own(0, range(chunks))
    has_low, has_high = lat > 0, lat < bands - 1

    @pl.when(has_high)
    def _():
        halo_copy(1).start()

    @pl.when(has_low)
    def _():
        halo_copy(-1).start()

    for chunk in range(chunks):
        for i1 in range(1, n1):
            arrive(0, i1, 0, [chunk])
        send_own(1, [chunk])


    @pl.when(has_low)
    def _():
        halo_copy(1).wait_recv()

    @pl.when(jnp.logical_not(has_low))
    def _():
        raw[0:rows] = jnp.zeros((rows, cols, chans), jnp.bfloat16)

    @pl.when(has_high)
    def _():
        halo_copy(-1).wait_recv()

    @pl.when(jnp.logical_not(has_high))
    def _():
        raw[2 * rows : 3 * rows] = jnp.zeros((rows, cols, chans), jnp.bfloat16)

    scale_rows(2 * rows, lambda r: r + rows * (r // rows))

    code = jnp.int32(0)
    combo = me * 2 + core
    for index, value in enumerate(codes):
        code = jnp.where(combo == index, jnp.int32(value), code)

    def stage_waits(w, stage):
        i1, i2 = offsets[stage]
        if stage == 0:
            locals_[1 + w].wait()
            return
        if legs(i1, i2) > legs(*offsets[stage - 1]):
            if w == 0 and legs(i1, i2) == 2:
                for o1 in range(1, n1):
                    arrive(1, o1, 0)
            for o1, o2 in offsets:
                if legs(o1, o2) == legs(i1, i2) and o2 > 0:
                    arrive(w, o1, o2)
        for chunk in range(chunks):
            sib_copy(w, *((i2, i1) if n2 > 1 else (i1, i2)), chunk).wait_recv()

    def conv(w, field, total, count, base):
        buf = (wb1, wb2)[w]

        def step(i, left_code):
            done = 0
            for at in range(TAPS):
                due = list(range(done, stage_of[at] + 1))
                done = max(done, stage_of[at] + 1)
                if due:

                    @pl.when(i == at)
                    def _():
                        for stage in due:
                            stage_waits(w, stage)

            tap = lax.rem(left_code, TAPS)
            dy, dx = tap // 3, lax.rem(tap, 3)
            left = field[dx, pl.ds(base + dy, count)].reshape(count * cols, chans)
            right = buf[pl.ds(pl.multiple_of(tap * chans, 128), chans), :]
            total[...] += jnp.dot(left, right, preferred_element_type=jnp.float32)
            return left_code // TAPS

        lax.fori_loop(0, TAPS, step, code)
        if w == 0 and n2 == 1:
            for o1 in range(1, n1):
                arrive(1, o1, 0)

    conv(0, sh, acc, rows + 2, rows - 2)
    @pl.loop(0, (rows + 2) * strips)
    def _(index):
        row, lanes = index // strips, lanes_of(index)
        at = pl.ds(pl.multiple_of(row * cols, cols), cols)
        value = jax.nn.gelu(acc[at, lanes], approximate=True)
        inside = jnp.logical_and(
            jnp.logical_or(row > 0, has_low), jnp.logical_or(row < rows + 1, has_high)
        )
        put_shifted(ish, row, lanes, jnp.where(inside, value, 0.0))

    conv(1, ish, acc2, rows, 0)

    own = sh[1, pl.ds(rows, rows)].reshape(rows * cols, chans).astype(jnp.float32)
    block = (own + acc2[...]).astype(jnp.bfloat16)
    pred = lax.dot_general(
        head[...], block, (((1,), (1,)), ((), ())), preferred_element_type=jnp.float32
    )
    pred = jnp.concatenate([pred[:, r * cols : (r + 1) * cols] for r in range(rows)], axis=0)
    preds[me] = pred.astype(jnp.bfloat16)

    pred_copies = [
        pltpu.make_async_remote_copy(
            src_ref=preds.at[me],
            dst_ref=preds.at[me],
            send_sem=pred_send.at[j],
            recv_sem=pred_recv.at[j],
            device_id=(lax.rem(me + j, members), lat),
            device_id_type=MESH,
        )
        for j in range(1, members)
    ]
    for copy in pred_copies:
        copy.start()
    for copy in pred_copies:
        copy.wait_recv()

    eps = 0.05 / members
    factor = (1.0 - eps) / (2.0 * members * (members - 1))
    truth = jnp.concatenate([target[:, r, :] for r in range(rows)], axis=0)
    all_preds = [preds[m].astype(jnp.float32) for m in range(members)]
    skill = sum(jnp.abs(p - truth) for p in all_preds) / members
    pairs = sum(
        jnp.abs(all_preds[m] - all_preds[n]) for m in range(members) for n in range(m)
    )
    score = skill - (2.0 * factor) * pairs
    weighted = jnp.zeros((fields, 128), jnp.float32)
    for r in range(rows):
        piece = score[r * fields : (r + 1) * fields]
        score_ref[:, r, :] = piece
        piece = sum(piece[:, c : c + 128] for c in range(0, cols, 128))
        weighted = weighted + piece * areas[r]
    parts[lat] = weighted

    part_copies = [
        pltpu.make_async_remote_copy(
            src_ref=parts.at[lat],
            dst_ref=parts.at[lat],
            send_sem=part_send.at[j],
            recv_sem=part_recv.at[j],
            device_id=(me, lax.rem(lat + j, bands)),
            device_id_type=MESH,
        )
        for j in range(1, bands)
    ]
    for copy in part_copies:
        copy.start()
    for copy in part_copies:
        copy.wait_recv()
    total = jnp.sum(parts[...], axis=0)
    total = jnp.sum(jnp.sum(total, axis=0, keepdims=True), axis=1, keepdims=True)
    mean = total / (fields * cols * area_total)
    mean_ref[0, 0] = mean[0, 0]

    @pl.when(has_high)
    def _():
        halo_copy(1).wait_send()

    @pl.when(has_low)
    def _():
        halo_copy(-1).wait_send()

    for w in range(2):
        for i1, i2 in offsets[1:]:
            for chunk in range(chunks):
                leg_copy(w, i1, i2, chunk).wait_send()
                sib_copy(w, i1, i2, chunk).wait_send()
    for copy in pred_copies + part_copies:
        copy.wait_send()


def body(members, bands, *args):
    states, head = args[0], args[5]
    rows, cols, chans = states.shape[1:]
    fields = head.shape[1]
    args = args[:5] + (head.T,) + args[6:]
    n1, n2 = route(members)
    chunks = chunk_count(args[3].shape[0])
    hbm = pl.BlockSpec(memory_space=pltpu.HBM)
    vmem = pl.BlockSpec(memory_space=pltpu.VMEM)
    smem = pl.BlockSpec(memory_space=pltpu.SMEM)
    dma = pltpu.SemaphoreType.DMA
    bf16, f32 = jnp.bfloat16, jnp.float32
    score, mean = pl.pallas_call(
        functools.partial(kernel, members, bands),
        out_shape=(
            jax.ShapeDtypeStruct((fields, rows, cols), f32),
            jax.ShapeDtypeStruct((1, 1), f32),
        ),
        in_specs=[hbm] * 8,
        out_specs=(vmem, smem),
        scratch_shapes=[
            pltpu.SMEM((1,), jnp.int32),
            pltpu.VMEM(args[2].shape, f32),
            pltpu.VMEM((fields, chans), bf16),
            pltpu.VMEM(args[6].shape, f32),
            pltpu.SMEM((1,), jnp.int32),
            pltpu.VMEM((8, chans), f32),
            pltpu.VMEM((3 * rows, cols, chans), bf16),
            pltpu.VMEM((3, 3 * rows, cols, chans), bf16),
            pltpu.VMEM((3, rows + 2, cols, chans), bf16),
            pltpu.VMEM((TAPS * chans, chans), bf16),
            pltpu.VMEM((TAPS * chans, chans), bf16),
            pltpu.VMEM(((rows + 2) * cols, chans), f32),
            pltpu.VMEM((rows * cols, chans), f32),
            pltpu.VMEM((members, rows * fields, cols), bf16),
            pltpu.VMEM((bands, fields, 128), f32),
            dma((8,)),
            dma((2,)),
            dma((2,)),
            dma((2, n1, n2, chunks)),
            dma((2, n1, n2, chunks)),
            dma((2, n1, n2, chunks)),
            dma((2, n1, n2, chunks)),
            dma((members,)),
            dma((members,)),
            dma((bands,)),
            dma((bands,)),
        ],
        compiler_params=pltpu.CompilerParams(
            collective_id=0, has_side_effects=True, vmem_limit_bytes=62 * 1024 * 1024
        ),
        cost_estimate=pl.CostEstimate(
            flops=2 * 6 * cols * TAPS * chans * chans,
            bytes_accessed=4 * TAPS * chans * chans,
            transcendentals=4 * cols * chans,
        ),
    )(*args)
    return score, mean[0, 0]


def solution(mesh):
    placed = (
        P("member", "lat", None, None),
        P("member"),
        P(),
        P("member", None),
        P("member", None),
        P(),
        P(None, "lat", None),
        P(),
    )
    return jax.shard_map(
        functools.partial(body, mesh.shape["member"], mesh.shape["lat"]),
        mesh=mesh,
        in_specs=placed,
        out_specs=(P(None, "lat", None), P()),
        check_vma=False,
    )
```

```python
import functools
import math

import jax
import jax.numpy as jnp
import numpy as np
from jax import lax
from jax.experimental import pallas as pl
from jax.experimental.pallas import tpu as pltpu
from jax.sharding import PartitionSpec as P

MESH = pl.DeviceIdType.MESH
TAPS = 9
ROWTAPS = 3


def route(members):
    side = math.isqrt(members)
    return (side, side) if side * side == members else (members, 1)


def legs(i1, i2):
    return (i1 > 0) + (i2 > 0)


def tap_plan(members, chans):
    n1, n2 = route(members)
    shard = TAPS * chans // members
    offsets = sorted(
        ((i1, i2) for i1 in range(n1) for i2 in range(n2)), key=lambda o: legs(*o)
    )
    codes, stages = [], []
    for me in range(members):
        for core in range(2):
            u, v = (1 + core * (n1 - 1), n1 - core * (n1 - 1)) if n2 > 1 else (1, members)
            p1, p2 = (me // u) % n1, (me // v) % n2
            arrival = {}
            for stage, (i1, i2) in enumerate(offsets):
                arrival[((p1 - i1) % n1) * u + ((p2 - i2) % n2) * v] = stage
            deep = ROWTAPS * chans
            need = [
                max(arrival[s] for s in range(g * deep // shard, ((g + 1) * deep - 1) // shard + 1))
                for g in range(ROWTAPS)
            ]
            order = sorted(range(ROWTAPS), key=lambda g: need[g])
            codes.append(sum(g * ROWTAPS**i for i, g in enumerate(order)))
            stages.append([need[g] for g in order])
    return offsets, codes, np.max(np.array(stages), axis=0).tolist()


def chunk_count(shard):
    return 2 if shard % 64 == 0 else 1


def kernel(
    members, bands, states, ident_hbm, gains_hbm, w1, w2, head_hbm, target_hbm, first_row_hbm,
    score_ref, mean_ref, ident, gains, head, target, first_row, gain_ref, raw, sh, ish, wb1, wb2, acc, acc2, preds, parts,
    local_sem, halo_send, halo_recv, leg_send, leg_recv, sib_send, sib_recv,
    pred_send, pred_recv, part_send, part_recv,
):
    rows, cols, chans = states.shape[1:]
    fields = head_hbm.shape[0]
    shard = w1.shape[0]
    n1, n2 = route(members)
    offsets, codes, stage_of = tap_plan(members, chans)
    me = lax.axis_index("member")
    lat = lax.axis_index("lat")
    core = lax.rem(lat, 2)
    sibling = lat + 1 - 2 * core

    barrier = pltpu.get_barrier_semaphore()
    for j in range(1, members):
        pl.semaphore_signal(
            barrier, inc=1, device_id=(lax.rem(me + j, members), lat), device_id_type=MESH
        )
    for j in range(1, bands):
        pl.semaphore_signal(
            barrier, inc=1, device_id=(me, lax.rem(lat + j, bands)), device_id_type=MESH
        )

    own_rows = pl.ds(pl.multiple_of(me * shard, 16), shard)
    locals_ = [
        pltpu.make_async_copy(states.at[0], raw.at[pl.ds(rows, rows)], local_sem.at[0]),
        pltpu.make_async_copy(w1, wb1.at[own_rows], local_sem.at[1]),
        pltpu.make_async_copy(w2, wb2.at[own_rows], local_sem.at[2]),
    ]
    small = [
        pltpu.make_async_copy(source, place, local_sem.at[3 + index])
        for index, (source, place) in enumerate(
            (
                (ident_hbm, ident),
                (gains_hbm, gains),
                (first_row_hbm, first_row),
                (head_hbm, head),
                (target_hbm, target),
            )
        )
    ]
    for copy in small + locals_:
        copy.start()
    for copy in small:
        copy.wait()

    lane = lax.broadcasted_iota(jnp.int32, gains.shape, 0)
    gain = jnp.sum(jnp.where(lane == ident[0], gains[...], 0.0), axis=0, keepdims=True)

    all_rows = rows * bands
    width = -(-all_rows // 128) * 128
    ids = lax.broadcasted_iota(jnp.int32, (8, width), 1)
    area_all = jnp.cos(jnp.pi * (90.0 - 0.1 * (first_row[0] + ids).astype(jnp.float32)) / 180.0)

    def area_sum(chosen):
        return jnp.sum(jnp.where(chosen, area_all, 0.0)[0:1], axis=1, keepdims=True)

    area_total = area_sum(ids < all_rows)
    areas = [area_sum(ids == lat * rows + r) for r in range(rows)]

    strip = 128
    strips = chans // strip
    place_ids = lax.broadcasted_iota(jnp.int32, (cols, strip), 0)

    def lanes_of(index):
        return pl.ds(pl.multiple_of(lax.rem(index, strips) * strip, strip), strip)

    def put_shifted(ref, row, lanes, value):
        low = jnp.where(place_ids == 0, 0.0, pltpu.roll(value, 1, 0))
        high = jnp.where(place_ids == cols - 1, 0.0, pltpu.roll(value, cols - 1, 0))
        for dx, part in enumerate((low, value, high)):
            place = pl.ds(pl.multiple_of(dx * chans + lanes.start, strip), strip)
            ref[row, :, place] = part.astype(jnp.bfloat16)

    def scale_rows(count, place):
        @pl.loop(0, count * strips)
        def _(index):
            row, lanes = place(index // strips), lanes_of(index)
            value = raw[row, :, lanes].astype(jnp.float32) * gain_ref[0:1, lanes]
            put_shifted(sh, row, lanes, value)

    gain_ref[...] = jnp.broadcast_to(gain, gain_ref.shape)
    locals_[0].wait()
    scale_rows(rows, lambda r: r + rows)
    acc[...] = jnp.zeros_like(acc)
    acc2[...] = jnp.zeros_like(acc2)

    pl.semaphore_wait(barrier, members - 1 + bands - 1)

    if n2 > 1:
        u, v = 1 + core * (n1 - 1), n1 - core * (n1 - 1)
    else:
        u, v = 1, members
    p1 = lax.rem(me // u, n1)
    p2 = lax.rem(me // v, n2)

    def member_at(q1, q2):
        return q1 * u + q2 * v

    def back(i1, i2):
        return member_at(lax.rem(p1 - i1 + n1, n1), lax.rem(p2 - i2 + n2, n2))

    chunks = chunk_count(shard)

    def half(ref, base, which, chunk):
        if shard % (32 * chunks) == 0:
            size = shard // (2 * chunks)
            first = base + which * (shard // 2) + chunk * size
            return ref.at[pl.ds(pl.multiple_of(first, 16), size)]
        span = ref.shape[1] // 2
        return ref.at[
            pl.ds(pl.multiple_of(base, 16), shard), pl.ds(pl.multiple_of(which * span, 128), span)
        ]

    def leg_copy(w, i1, i2, chunk):
        src, buf = ((w1, wb1), (w2, wb2))[w]
        if i2 == 0:
            dest = member_at(lax.rem(p1 + i1, n1), p2)
            origin, j1 = me, 0
        else:
            dest = member_at(p1, lax.rem(p2 + i2, n2))
            origin, j1 = back(i1, 0), i1
        source = (
            half(src, 0, core, chunk) if j1 == 0 else half(buf, origin * shard, core, chunk)
        )
        return pltpu.make_async_remote_copy(
            src_ref=source,
            dst_ref=half(buf, origin * shard, core, chunk),
            send_sem=leg_send.at[w, i1, i2, chunk],
            recv_sem=leg_recv.at[w, i1, i2, chunk],
            device_id=(dest, lat),
            device_id_type=MESH,
        )

    def sib_copy(w, i1, i2, chunk):
        buf = (wb1, wb2)[w]
        place = half(buf, back(i1, i2) * shard, core, chunk)
        return pltpu.make_async_remote_copy(
            src_ref=place,
            dst_ref=place,
            send_sem=sib_send.at[w, i1, i2, chunk],
            recv_sem=sib_recv.at[w, i1, i2, chunk],
            device_id=(me, sibling),
            device_id_type=MESH,
        )

    def send_own(w, some):
        for chunk in some:
            for i1 in range(1, n1):
                leg_copy(w, i1, 0, chunk).start()
            for i2 in range(1, n2):
                leg_copy(w, 0, i2, chunk).start()

    def arrive(w, i1, i2, some=range(chunks)):
        for chunk in some:
            leg_copy(w, i1, i2, chunk).wait_recv()
            if i2 == 0:
                for j2 in range(1, n2):
                    leg_copy(w, i1, j2, chunk).start()
            sib_copy(w, i1, i2, chunk).start()

    def halo_copy(step):
        place = pl.ds(0, rows) if step > 0 else pl.ds(2 * rows, rows)
        index = 0 if step > 0 else 1
        return pltpu.make_async_remote_copy(
            src_ref=states.at[0],
            dst_ref=raw.at[place],
            send_sem=halo_send.at[index],
            recv_sem=halo_recv.at[index],
            device_id=(me, lat + step),
            device_id_type=MESH,
        )

    send_own(0, range(chunks))
    has_low, has_high = lat > 0, lat < bands - 1

    @pl.when(has_high)
    def _():
        halo_copy(1).start()

    @pl.when(has_low)
    def _():
        halo_copy(-1).start()

    for chunk in range(chunks):
        for i1 in range(1, n1):
            arrive(0, i1, 0, [chunk])
        send_own(1, [chunk])


    @pl.when(has_low)
    def _():
        halo_copy(1).wait_recv()

    @pl.when(jnp.logical_not(has_low))
    def _():
        raw[0:rows] = jnp.zeros((rows, cols, chans), jnp.bfloat16)

    @pl.when(has_high)
    def _():
        halo_copy(-1).wait_recv()

    @pl.when(jnp.logical_not(has_high))
    def _():
        raw[2 * rows : 3 * rows] = jnp.zeros((rows, cols, chans), jnp.bfloat16)

    scale_rows(2 * rows, lambda r: r + rows * (r // rows))

    code = jnp.int32(0)
    combo = me * 2 + core
    for index, value in enumerate(codes):
        code = jnp.where(combo == index, jnp.int32(value), code)

    def stage_waits(w, stage):
        i1, i2 = offsets[stage]
        if stage == 0:
            locals_[1 + w].wait()
            return
        if legs(i1, i2) > legs(*offsets[stage - 1]):
            if w == 0 and legs(i1, i2) == 2:
                for o1 in range(1, n1):
                    arrive(1, o1, 0)
            for o1, o2 in offsets:
                if legs(o1, o2) == legs(i1, i2) and o2 > 0:
                    arrive(w, o1, o2)
        for chunk in range(chunks):
            sib_copy(w, *((i2, i1) if n2 > 1 else (i1, i2)), chunk).wait_recv()

    def conv(w, field, total, count, base):
        buf = (wb1, wb2)[w]

        def step(i, left_code):
            done = 0
            for at in range(ROWTAPS):
                due = list(range(done, stage_of[at] + 1))
                done = max(done, stage_of[at] + 1)
                if due:

                    @pl.when(i == at)
                    def _():
                        for stage in due:
                            stage_waits(w, stage)

            deep = ROWTAPS * chans
            dy = lax.rem(left_code, ROWTAPS)
            left = field[pl.ds(base + dy, count)].reshape(count * cols, deep)
            right = buf[pl.ds(pl.multiple_of(dy * deep, 128), deep), :]
            total[...] += jnp.dot(left, right, preferred_element_type=jnp.float32)
            return left_code // ROWTAPS

        lax.fori_loop(0, ROWTAPS, step, code)
        if w == 0 and n2 == 1:
            for o1 in range(1, n1):
                arrive(1, o1, 0)

    conv(0, sh, acc, rows + 2, rows - 2)
    @pl.loop(0, (rows + 2) * strips)
    def _(index):
        row, lanes = index // strips, lanes_of(index)
        at = pl.ds(pl.multiple_of(row * cols, cols), cols)
        value = jax.nn.gelu(acc[at, lanes], approximate=True)
        inside = jnp.logical_and(
            jnp.logical_or(row > 0, has_low), jnp.logical_or(row < rows + 1, has_high)
        )
        put_shifted(ish, row, lanes, jnp.where(inside, value, 0.0))

    conv(1, ish, acc2, rows, 0)

    own = sh[pl.ds(rows, rows), :, pl.ds(chans, chans)].reshape(rows * cols, chans).astype(jnp.float32)
    block = (own + acc2[...]).astype(jnp.bfloat16)
    pred = lax.dot_general(
        head[...], block, (((1,), (1,)), ((), ())), preferred_element_type=jnp.float32
    )
    pred = jnp.concatenate([pred[:, r * cols : (r + 1) * cols] for r in range(rows)], axis=0)
    preds[me] = pred.astype(jnp.bfloat16)

    pred_copies = [
        pltpu.make_async_remote_copy(
            src_ref=preds.at[me],
            dst_ref=preds.at[me],
            send_sem=pred_send.at[j],
            recv_sem=pred_recv.at[j],
            device_id=(lax.rem(me + j, members), lat),
            device_id_type=MESH,
        )
        for j in range(1, members)
    ]
    for copy in pred_copies:
        copy.start()
    for copy in pred_copies:
        copy.wait_recv()

    eps = 0.05 / members
    factor = (1.0 - eps) / (2.0 * members * (members - 1))
    truth = jnp.concatenate([target[:, r, :] for r in range(rows)], axis=0)
    all_preds = [preds[m].astype(jnp.float32) for m in range(members)]
    skill = sum(jnp.abs(p - truth) for p in all_preds) / members
    pairs = sum(
        jnp.abs(all_preds[m] - all_preds[n]) for m in range(members) for n in range(m)
    )
    score = skill - (2.0 * factor) * pairs
    weighted = jnp.zeros((fields, 128), jnp.float32)
    for r in range(rows):
        piece = score[r * fields : (r + 1) * fields]
        score_ref[:, r, :] = piece
        piece = sum(piece[:, c : c + 128] for c in range(0, cols, 128))
        weighted = weighted + piece * areas[r]
    parts[lat] = weighted

    part_copies = [
        pltpu.make_async_remote_copy(
            src_ref=parts.at[lat],
            dst_ref=parts.at[lat],
            send_sem=part_send.at[j],
            recv_sem=part_recv.at[j],
            device_id=(me, lax.rem(lat + j, bands)),
            device_id_type=MESH,
        )
        for j in range(1, bands)
    ]
    for copy in part_copies:
        copy.start()
    for copy in part_copies:
        copy.wait_recv()
    total = jnp.sum(parts[...], axis=0)
    total = jnp.sum(jnp.sum(total, axis=0, keepdims=True), axis=1, keepdims=True)
    mean = total / (fields * cols * area_total)
    mean_ref[0, 0] = mean[0, 0]

    @pl.when(has_high)
    def _():
        halo_copy(1).wait_send()

    @pl.when(has_low)
    def _():
        halo_copy(-1).wait_send()

    for w in range(2):
        for i1, i2 in offsets[1:]:
            for chunk in range(chunks):
                leg_copy(w, i1, i2, chunk).wait_send()
                sib_copy(w, i1, i2, chunk).wait_send()
    for copy in pred_copies + part_copies:
        copy.wait_send()


def body(members, bands, *args):
    states, head = args[0], args[5]
    rows, cols, chans = states.shape[1:]
    fields = head.shape[1]
    args = args[:5] + (head.T,) + args[6:]
    n1, n2 = route(members)
    chunks = chunk_count(args[3].shape[0])
    hbm = pl.BlockSpec(memory_space=pltpu.HBM)
    vmem = pl.BlockSpec(memory_space=pltpu.VMEM)
    smem = pl.BlockSpec(memory_space=pltpu.SMEM)
    dma = pltpu.SemaphoreType.DMA
    bf16, f32 = jnp.bfloat16, jnp.float32
    score, mean = pl.pallas_call(
        functools.partial(kernel, members, bands),
        out_shape=(
            jax.ShapeDtypeStruct((fields, rows, cols), f32),
            jax.ShapeDtypeStruct((1, 1), f32),
        ),
        in_specs=[hbm] * 8,
        out_specs=(vmem, smem),
        scratch_shapes=[
            pltpu.SMEM((1,), jnp.int32),
            pltpu.VMEM(args[2].shape, f32),
            pltpu.VMEM((fields, chans), bf16),
            pltpu.VMEM(args[6].shape, f32),
            pltpu.SMEM((1,), jnp.int32),
            pltpu.VMEM((8, chans), f32),
            pltpu.VMEM((3 * rows, cols, chans), bf16),
            pltpu.VMEM((3 * rows, cols, ROWTAPS * chans), bf16),
            pltpu.VMEM((rows + 2, cols, ROWTAPS * chans), bf16),
            pltpu.VMEM((TAPS * chans, chans), bf16),
            pltpu.VMEM((TAPS * chans, chans), bf16),
            pltpu.VMEM(((rows + 2) * cols, chans), f32),
            pltpu.VMEM((rows * cols, chans), f32),
            pltpu.VMEM((members, rows * fields, cols), bf16),
            pltpu.VMEM((bands, fields, 128), f32),
            dma((8,)),
            dma((2,)),
            dma((2,)),
            dma((2, n1, n2, chunks)),
            dma((2, n1, n2, chunks)),
            dma((2, n1, n2, chunks)),
            dma((2, n1, n2, chunks)),
            dma((members,)),
            dma((members,)),
            dma((bands,)),
            dma((bands,)),
        ],
        compiler_params=pltpu.CompilerParams(
            collective_id=0, has_side_effects=True, vmem_limit_bytes=62 * 1024 * 1024
        ),
        cost_estimate=pl.CostEstimate(
            flops=2 * 6 * cols * TAPS * chans * chans,
            bytes_accessed=4 * TAPS * chans * chans,
            transcendentals=4 * cols * chans,
        ),
    )(*args)
    return score, mean[0, 0]


def solution(mesh):
    placed = (
        P("member", "lat", None, None),
        P("member"),
        P(),
        P("member", None),
        P("member", None),
        P(),
        P(None, "lat", None),
        P(),
    )
    return jax.shard_map(
        functools.partial(body, mesh.shape["member"], mesh.shape["lat"]),
        mesh=mesh,
        in_specs=placed,
        out_specs=(P(None, "lat", None), P()),
        check_vma=False,
    )
```

```python
import functools
import math

import jax
import jax.numpy as jnp
import numpy as np
from jax import lax
from jax.experimental import pallas as pl
from jax.experimental.pallas import tpu as pltpu
from jax.sharding import PartitionSpec as P

MESH = pl.DeviceIdType.MESH
TAPS = 9
ROWTAPS = 3


def route(members):
    side = math.isqrt(members)
    return (side, side) if side * side == members else (members, 1)


def legs(i1, i2):
    return (i1 > 0) + (i2 > 0)


def tap_plan(members, chans):
    n1, n2 = route(members)
    shard = TAPS * chans // members
    offsets = sorted(
        ((i1, i2) for i1 in range(n1) for i2 in range(n2)), key=lambda o: legs(*o)
    )
    codes, stages = [], []
    for me in range(members):
        for core in range(2):
            u, v = (1 + core * (n1 - 1), n1 - core * (n1 - 1)) if n2 > 1 else (1, members)
            p1, p2 = (me // u) % n1, (me // v) % n2
            arrival = {}
            for stage, (i1, i2) in enumerate(offsets):
                arrival[((p1 - i1) % n1) * u + ((p2 - i2) % n2) * v] = stage
            deep = ROWTAPS * chans
            need = [
                max(arrival[s] for s in range(g * deep // shard, ((g + 1) * deep - 1) // shard + 1))
                for g in range(ROWTAPS)
            ]
            order = sorted(range(ROWTAPS), key=lambda g: need[g])
            codes.append(sum(g * ROWTAPS**i for i, g in enumerate(order)))
            stages.append([need[g] for g in order])
    return offsets, codes, np.max(np.array(stages), axis=0).tolist()


def shared_rows(shard, bands):
    return shard // 9 if shard % 144 == 0 and shard % 32 == 0 and bands % 4 == 0 else 0


def kernel(
    members, bands, states, ident_hbm, gains_hbm, w1, w2, head_hbm, target_hbm, first_row_hbm,
    score_ref, mean_ref, ident, gains, head, target, first_row, gain_ref, raw, sh, ish, wb1, wb2, acc, acc2, preds, parts,
    local_sem, halo_send, halo_recv, leg_send, leg_recv, sib_send, sib_recv, plane_send, plane_recv,
    pred_send, pred_recv, part_send, part_recv,
):
    rows, cols, chans = states.shape[1:]
    fields = head_hbm.shape[0]
    shard = w1.shape[0]
    n1, n2 = route(members)
    offsets, codes, stage_of = tap_plan(members, chans)
    me = lax.axis_index("member")
    lat = lax.axis_index("lat")
    core = lax.rem(lat, 2)
    sibling = lat + 1 - 2 * core

    barrier = pltpu.get_barrier_semaphore()
    for j in range(1, members):
        pl.semaphore_signal(
            barrier, inc=1, device_id=(lax.rem(me + j, members), lat), device_id_type=MESH
        )
    for j in range(1, bands):
        pl.semaphore_signal(
            barrier, inc=1, device_id=(me, lax.rem(lat + j, bands)), device_id_type=MESH
        )

    own_rows = pl.ds(pl.multiple_of(me * shard, 16), shard)
    locals_ = [
        pltpu.make_async_copy(states.at[0], raw.at[pl.ds(rows, rows)], local_sem.at[0]),
        pltpu.make_async_copy(w1, wb1.at[own_rows], local_sem.at[1]),
        pltpu.make_async_copy(w2, wb2.at[own_rows], local_sem.at[2]),
    ]
    small = [
        pltpu.make_async_copy(source, place, local_sem.at[3 + index])
        for index, (source, place) in enumerate(
            (
                (ident_hbm, ident),
                (gains_hbm, gains),
                (first_row_hbm, first_row),
                (head_hbm, head),
                (target_hbm, target),
            )
        )
    ]
    for copy in small + locals_:
        copy.start()
    for copy in small:
        copy.wait()

    lane = lax.broadcasted_iota(jnp.int32, gains.shape, 0)
    gain = jnp.sum(jnp.where(lane == ident[0], gains[...], 0.0), axis=0, keepdims=True)

    all_rows = rows * bands
    width = -(-all_rows // 128) * 128
    ids = lax.broadcasted_iota(jnp.int32, (8, width), 1)
    area_all = jnp.cos(jnp.pi * (90.0 - 0.1 * (first_row[0] + ids).astype(jnp.float32)) / 180.0)

    def area_sum(chosen):
        return jnp.sum(jnp.where(chosen, area_all, 0.0)[0:1], axis=1, keepdims=True)

    area_total = area_sum(ids < all_rows)
    areas = [area_sum(ids == lat * rows + r) for r in range(rows)]

    strip = 128
    strips = chans // strip
    place_ids = lax.broadcasted_iota(jnp.int32, (cols, strip), 0)

    def lanes_of(index):
        return pl.ds(pl.multiple_of(lax.rem(index, strips) * strip, strip), strip)

    def put_shifted(ref, row, lanes, value):
        low = jnp.where(place_ids == 0, 0.0, pltpu.roll(value, 1, 0))
        high = jnp.where(place_ids == cols - 1, 0.0, pltpu.roll(value, cols - 1, 0))
        for dx, part in enumerate((low, value, high)):
            place = pl.ds(pl.multiple_of(dx * chans + lanes.start, strip), strip)
            ref[row, :, place] = part.astype(jnp.bfloat16)

    def scale_rows(count, place):
        @pl.loop(0, count * strips)
        def _(index):
            row, lanes = place(index // strips), lanes_of(index)
            value = raw[row, :, lanes].astype(jnp.float32) * gain_ref[0:1, lanes]
            put_shifted(sh, row, lanes, value)

    gain_ref[...] = jnp.broadcast_to(gain, gain_ref.shape)
    locals_[0].wait()
    scale_rows(rows, lambda r: r + rows)
    acc[...] = jnp.zeros_like(acc)
    acc2[...] = jnp.zeros_like(acc2)

    pl.semaphore_wait(barrier, members - 1 + bands - 1)

    if n2 > 1:
        u, v = 1 + core * (n1 - 1), n1 - core * (n1 - 1)
    else:
        u, v = 1, members
    p1 = lax.rem(me // u, n1)
    p2 = lax.rem(me // v, n2)

    def member_at(q1, q2):
        return q1 * u + q2 * v

    def back(i1, i2):
        return member_at(lax.rem(p1 - i1 + n1, n1), lax.rem(p2 - i2 + n2, n2))

    shared = shared_rows(shard, bands)
    chunks = 2 if shared else 1
    passed = 3 if shared else 1
    parity = lax.rem(lat // 2, 2)
    partner = lat + 2 - 4 * parity

    def half(ref, base, which, chunk):
        if shared:
            first = base + which * (shard // 2)
            first += (parity * shared, 2 * shared, (1 - parity) * shared)[chunk]
            size = (shared, shard // 2 - 2 * shared, shared)[chunk]
            return ref.at[pl.ds(pl.multiple_of(first, 16), size)]
        span = ref.shape[1] // 2
        return ref.at[
            pl.ds(pl.multiple_of(base, 16), shard), pl.ds(pl.multiple_of(which * span, 128), span)
        ]

    def leg_copy(w, i1, i2, chunk):
        src, buf = ((w1, wb1), (w2, wb2))[w]
        if i2 == 0:
            dest = member_at(lax.rem(p1 + i1, n1), p2)
            origin, j1 = me, 0
        else:
            dest = member_at(p1, lax.rem(p2 + i2, n2))
            origin, j1 = back(i1, 0), i1
        source = (
            half(src, 0, core, chunk) if j1 == 0 else half(buf, origin * shard, core, chunk)
        )
        return pltpu.make_async_remote_copy(
            src_ref=source,
            dst_ref=half(buf, origin * shard, core, chunk),
            send_sem=leg_send.at[w, i1, i2, chunk],
            recv_sem=leg_recv.at[w, i1, i2, chunk],
            device_id=(dest, lat),
            device_id_type=MESH,
        )

    def sib_copy(w, i1, i2, chunk):
        buf = (wb1, wb2)[w]
        place = half(buf, back(i1, i2) * shard, core, chunk)
        return pltpu.make_async_remote_copy(
            src_ref=place,
            dst_ref=place,
            send_sem=sib_send.at[w, i1, i2, chunk],
            recv_sem=sib_recv.at[w, i1, i2, chunk],
            device_id=(me, sibling),
            device_id_type=MESH,
        )

    def plane_copy(w, i1, i2, chunk):
        buf = (wb1, wb2)[w]
        place = half(buf, back(i1, i2) * shard, core, chunk)
        return pltpu.make_async_remote_copy(
            src_ref=place,
            dst_ref=place,
            send_sem=plane_send.at[w, i1, i2],
            recv_sem=plane_recv.at[w, i1, i2],
            device_id=(me, partner),
            device_id_type=MESH,
        )

    def plane_arrive(w, i1, i2):
        if shared:
            plane_copy(w, i1, i2, 2).wait_recv()
            sib_copy(w, i1, i2, 2).start()

    def send_own(w, some):
        for chunk in some:
            for i1 in range(1, n1):
                leg_copy(w, i1, 0, chunk).start()
            for i2 in range(1, n2):
                leg_copy(w, 0, i2, chunk).start()

    def arrive(w, i1, i2, some=range(chunks)):
        for chunk in some:
            leg_copy(w, i1, i2, chunk).wait_recv()
            if i2 == 0:
                for j2 in range(1, n2):
                    leg_copy(w, i1, j2, chunk).start()
            if shared and chunk == 0:
                plane_copy(w, i1, i2, 0).start()
            sib_copy(w, i1, i2, chunk).start()

    def halo_copy(step):
        place = pl.ds(0, rows) if step > 0 else pl.ds(2 * rows, rows)
        index = 0 if step > 0 else 1
        return pltpu.make_async_remote_copy(
            src_ref=states.at[0],
            dst_ref=raw.at[place],
            send_sem=halo_send.at[index],
            recv_sem=halo_recv.at[index],
            device_id=(me, lat + step),
            device_id_type=MESH,
        )

    send_own(0, range(chunks))
    has_low, has_high = lat > 0, lat < bands - 1

    @pl.when(has_high)
    def _():
        halo_copy(1).start()

    @pl.when(has_low)
    def _():
        halo_copy(-1).start()

    for chunk in range(chunks):
        for i1 in range(1, n1):
            arrive(0, i1, 0, [chunk])
        send_own(1, [chunk])


    @pl.when(has_low)
    def _():
        halo_copy(1).wait_recv()

    @pl.when(jnp.logical_not(has_low))
    def _():
        raw[0:rows] = jnp.zeros((rows, cols, chans), jnp.bfloat16)

    @pl.when(has_high)
    def _():
        halo_copy(-1).wait_recv()

    @pl.when(jnp.logical_not(has_high))
    def _():
        raw[2 * rows : 3 * rows] = jnp.zeros((rows, cols, chans), jnp.bfloat16)

    scale_rows(2 * rows, lambda r: r + rows * (r // rows))

    code = jnp.int32(0)
    combo = me * 2 + core
    for index, value in enumerate(codes):
        code = jnp.where(combo == index, jnp.int32(value), code)

    def stage_waits(w, stage):
        i1, i2 = offsets[stage]
        if stage == 0:
            locals_[1 + w].wait()
            return
        if legs(i1, i2) > legs(*offsets[stage - 1]):
            if w == 0 and legs(i1, i2) == 2:
                for o1 in range(1, n1):
                    arrive(1, o1, 0)
            for o1, o2 in offsets:
                if legs(o1, o2) == legs(i1, i2) and o2 > 0:
                    arrive(w, o1, o2)
            for o1, o2 in offsets:
                if legs(o1, o2) == legs(i1, i2):
                    plane_arrive(w, o1, o2)
        for chunk in range(passed):
            sib_copy(w, *((i2, i1) if n2 > 1 else (i1, i2)), chunk).wait_recv()

    def conv(w, field, total, count, base):
        buf = (wb1, wb2)[w]

        def step(i, left_code):
            done = 0
            for at in range(ROWTAPS):
                due = list(range(done, stage_of[at] + 1))
                done = max(done, stage_of[at] + 1)
                if due:

                    @pl.when(i == at)
                    def _():
                        for stage in due:
                            stage_waits(w, stage)

            deep = ROWTAPS * chans
            dy = lax.rem(left_code, ROWTAPS)
            left = field[pl.ds(base + dy, count)].reshape(count * cols, deep)
            right = buf[pl.ds(pl.multiple_of(dy * deep, 128), deep), :]
            total[...] += jnp.dot(left, right, preferred_element_type=jnp.float32)
            return left_code // ROWTAPS

        lax.fori_loop(0, ROWTAPS, step, code)
        if w == 0 and n2 == 1:
            for o1 in range(1, n1):
                arrive(1, o1, 0)

    conv(0, sh, acc, rows + 2, rows - 2)
    @pl.loop(0, (rows + 2) * strips)
    def _(index):
        row, lanes = index // strips, lanes_of(index)
        at = pl.ds(pl.multiple_of(row * cols, cols), cols)
        value = jax.nn.gelu(acc[at, lanes], approximate=True)
        inside = jnp.logical_and(
            jnp.logical_or(row > 0, has_low), jnp.logical_or(row < rows + 1, has_high)
        )
        put_shifted(ish, row, lanes, jnp.where(inside, value, 0.0))

    conv(1, ish, acc2, rows, 0)

    own = sh[pl.ds(rows, rows), :, pl.ds(chans, chans)].reshape(rows * cols, chans).astype(jnp.float32)
    block = (own + acc2[...]).astype(jnp.bfloat16)
    pred = lax.dot_general(
        head[...], block, (((1,), (1,)), ((), ())), preferred_element_type=jnp.float32
    )
    pred = jnp.concatenate([pred[:, r * cols : (r + 1) * cols] for r in range(rows)], axis=0)
    preds[me] = pred.astype(jnp.bfloat16)

    pred_copies = [
        pltpu.make_async_remote_copy(
            src_ref=preds.at[me],
            dst_ref=preds.at[me],
            send_sem=pred_send.at[j],
            recv_sem=pred_recv.at[j],
            device_id=(lax.rem(me + j, members), lat),
            device_id_type=MESH,
        )
        for j in range(1, members)
    ]
    for copy in pred_copies:
        copy.start()
    for copy in pred_copies:
        copy.wait_recv()

    eps = 0.05 / members
    factor = (1.0 - eps) / (2.0 * members * (members - 1))
    truth = jnp.concatenate([target[:, r, :] for r in range(rows)], axis=0)
    all_preds = [preds[m].astype(jnp.float32) for m in range(members)]
    skill = sum(jnp.abs(p - truth) for p in all_preds) / members
    pairs = sum(
        jnp.abs(all_preds[m] - all_preds[n]) for m in range(members) for n in range(m)
    )
    score = skill - (2.0 * factor) * pairs
    weighted = jnp.zeros((fields, 128), jnp.float32)
    for r in range(rows):
        piece = score[r * fields : (r + 1) * fields]
        score_ref[:, r, :] = piece
        piece = sum(piece[:, c : c + 128] for c in range(0, cols, 128))
        weighted = weighted + piece * areas[r]
    parts[lat] = weighted

    part_copies = [
        pltpu.make_async_remote_copy(
            src_ref=parts.at[lat],
            dst_ref=parts.at[lat],
            send_sem=part_send.at[j],
            recv_sem=part_recv.at[j],
            device_id=(me, lax.rem(lat + j, bands)),
            device_id_type=MESH,
        )
        for j in range(1, bands)
    ]
    for copy in part_copies:
        copy.start()
    for copy in part_copies:
        copy.wait_recv()
    total = jnp.sum(parts[...], axis=0)
    total = jnp.sum(jnp.sum(total, axis=0, keepdims=True), axis=1, keepdims=True)
    mean = total / (fields * cols * area_total)
    mean_ref[0, 0] = mean[0, 0]

    @pl.when(has_high)
    def _():
        halo_copy(1).wait_send()

    @pl.when(has_low)
    def _():
        halo_copy(-1).wait_send()

    for w in range(2):
        for i1, i2 in offsets[1:]:
            for chunk in range(chunks):
                leg_copy(w, i1, i2, chunk).wait_send()
            for chunk in range(passed):
                sib_copy(w, i1, i2, chunk).wait_send()
            if shared:
                plane_copy(w, i1, i2, 0).wait_send()
    for copy in pred_copies + part_copies:
        copy.wait_send()


def body(members, bands, *args):
    states, head = args[0], args[5]
    rows, cols, chans = states.shape[1:]
    fields = head.shape[1]
    args = args[:5] + (head.T,) + args[6:]
    n1, n2 = route(members)
    hbm = pl.BlockSpec(memory_space=pltpu.HBM)
    vmem = pl.BlockSpec(memory_space=pltpu.VMEM)
    smem = pl.BlockSpec(memory_space=pltpu.SMEM)
    dma = pltpu.SemaphoreType.DMA
    bf16, f32 = jnp.bfloat16, jnp.float32
    score, mean = pl.pallas_call(
        functools.partial(kernel, members, bands),
        out_shape=(
            jax.ShapeDtypeStruct((fields, rows, cols), f32),
            jax.ShapeDtypeStruct((1, 1), f32),
        ),
        in_specs=[hbm] * 8,
        out_specs=(vmem, smem),
        scratch_shapes=[
            pltpu.SMEM((1,), jnp.int32),
            pltpu.VMEM(args[2].shape, f32),
            pltpu.VMEM((fields, chans), bf16),
            pltpu.VMEM(args[6].shape, f32),
            pltpu.SMEM((1,), jnp.int32),
            pltpu.VMEM((8, chans), f32),
            pltpu.VMEM((3 * rows, cols, chans), bf16),
            pltpu.VMEM((3 * rows, cols, ROWTAPS * chans), bf16),
            pltpu.VMEM((rows + 2, cols, ROWTAPS * chans), bf16),
            pltpu.VMEM((TAPS * chans, chans), bf16),
            pltpu.VMEM((TAPS * chans, chans), bf16),
            pltpu.VMEM(((rows + 2) * cols, chans), f32),
            pltpu.VMEM((rows * cols, chans), f32),
            pltpu.VMEM((members, rows * fields, cols), bf16),
            pltpu.VMEM((bands, fields, 128), f32),
            dma((8,)),
            dma((2,)),
            dma((2,)),
            dma((2, n1, n2, 2)),
            dma((2, n1, n2, 2)),
            dma((2, n1, n2, 3)),
            dma((2, n1, n2, 3)),
            dma((2, n1, n2)),
            dma((2, n1, n2)),
            dma((members,)),
            dma((members,)),
            dma((bands,)),
            dma((bands,)),
        ],
        compiler_params=pltpu.CompilerParams(
            collective_id=0, has_side_effects=True, vmem_limit_bytes=62 * 1024 * 1024
        ),
        cost_estimate=pl.CostEstimate(
            flops=2 * 6 * cols * TAPS * chans * chans,
            bytes_accessed=4 * TAPS * chans * chans,
            transcendentals=4 * cols * chans,
        ),
    )(*args)
    return score, mean[0, 0]


def solution(mesh):
    placed = (
        P("member", "lat", None, None),
        P("member"),
        P(),
        P("member", None),
        P("member", None),
        P(),
        P(None, "lat", None),
        P(),
    )
    return jax.shard_map(
        functools.partial(body, mesh.shape["member"], mesh.shape["lat"]),
        mesh=mesh,
        in_specs=placed,
        out_specs=(P(None, "lat", None), P()),
        check_vma=False,
    )
```

```python
import functools
import math

import jax
import jax.numpy as jnp
import numpy as np
from jax import lax
from jax.experimental import pallas as pl
from jax.experimental.pallas import tpu as pltpu
from jax.sharding import PartitionSpec as P

MESH = pl.DeviceIdType.MESH
TAPS = 9
ROWTAPS = 3


def route(members):
    side = math.isqrt(members)
    return (side, side) if side * side == members else (members, 1)


def legs(i1, i2):
    return (i1 > 0) + (i2 > 0)


def tap_plan(members, chans):
    n1, n2 = route(members)
    shard = TAPS * chans // members
    offsets = sorted(
        ((i1, i2) for i1 in range(n1) for i2 in range(n2)), key=lambda o: legs(*o)
    )
    codes, stages = [], []
    for me in range(members):
        for core in range(2):
            u, v = (1 + core * (n1 - 1), n1 - core * (n1 - 1)) if n2 > 1 else (1, members)
            p1, p2 = (me // u) % n1, (me // v) % n2
            arrival = {}
            for stage, (i1, i2) in enumerate(offsets):
                arrival[((p1 - i1) % n1) * u + ((p2 - i2) % n2) * v] = stage
            deep = ROWTAPS * chans
            need = [
                max(arrival[s] for s in range(g * deep // shard, ((g + 1) * deep - 1) // shard + 1))
                for g in range(ROWTAPS)
            ]
            order = sorted(range(ROWTAPS), key=lambda g: need[g])
            codes.append(sum(g * ROWTAPS**i for i, g in enumerate(order)))
            stages.append([need[g] for g in order])
    return offsets, codes, np.max(np.array(stages), axis=0).tolist()


def chunk_count(shard):
    return 1


def kernel(
    members, bands, states, ident_hbm, gains_hbm, w1, w2, head_hbm, target_hbm, first_row_hbm,
    score_ref, mean_ref, ident, gains, head, target, first_row, gain_ref, raw, sh, ish, wb1, wb2, acc, acc2, preds, parts,
    local_sem, halo_send, halo_recv, leg_send, leg_recv, sib_send, sib_recv,
    pred_send, pred_recv, part_send, part_recv,
):
    rows, cols, chans = states.shape[1:]
    fields = head_hbm.shape[0]
    shard = w1.shape[0]
    n1, n2 = route(members)
    offsets, codes, stage_of = tap_plan(members, chans)
    me = lax.axis_index("member")
    lat = lax.axis_index("lat")
    core = lax.rem(lat, 2)
    sibling = lat + 1 - 2 * core

    barrier = pltpu.get_barrier_semaphore()
    for j in range(1, members):
        pl.semaphore_signal(
            barrier, inc=1, device_id=(lax.rem(me + j, members), lat), device_id_type=MESH
        )
    for j in range(1, bands):
        pl.semaphore_signal(
            barrier, inc=1, device_id=(me, lax.rem(lat + j, bands)), device_id_type=MESH
        )

    own_rows = pl.ds(pl.multiple_of(me * shard, 16), shard)
    locals_ = [
        pltpu.make_async_copy(states.at[0], raw.at[pl.ds(rows, rows)], local_sem.at[0]),
        pltpu.make_async_copy(w1, wb1.at[own_rows], local_sem.at[1]),
        pltpu.make_async_copy(w2, wb2.at[own_rows], local_sem.at[2]),
    ]
    small = [
        pltpu.make_async_copy(source, place, local_sem.at[3 + index])
        for index, (source, place) in enumerate(
            (
                (ident_hbm, ident),
                (gains_hbm, gains),
                (first_row_hbm, first_row),
                (head_hbm, head),
                (target_hbm, target),
            )
        )
    ]
    for copy in small + locals_:
        copy.start()
    for copy in small:
        copy.wait()

    lane = lax.broadcasted_iota(jnp.int32, gains.shape, 0)
    gain = jnp.sum(jnp.where(lane == ident[0], gains[...], 0.0), axis=0, keepdims=True)

    all_rows = rows * bands
    width = -(-all_rows // 128) * 128
    ids = lax.broadcasted_iota(jnp.int32, (8, width), 1)
    area_all = jnp.cos(jnp.pi * (90.0 - 0.1 * (first_row[0] + ids).astype(jnp.float32)) / 180.0)

    def area_sum(chosen):
        return jnp.sum(jnp.where(chosen, area_all, 0.0)[0:1], axis=1, keepdims=True)

    area_total = area_sum(ids < all_rows)
    areas = [area_sum(ids == lat * rows + r) for r in range(rows)]

    strip = 128
    strips = chans // strip
    place_ids = lax.broadcasted_iota(jnp.int32, (cols, strip), 0)

    def lanes_of(index):
        return pl.ds(pl.multiple_of(lax.rem(index, strips) * strip, strip), strip)

    def put_shifted(ref, row, lanes, value):
        low = jnp.where(place_ids == 0, 0.0, pltpu.roll(value, 1, 0))
        high = jnp.where(place_ids == cols - 1, 0.0, pltpu.roll(value, cols - 1, 0))
        for dx, part in enumerate((low, value, high)):
            place = pl.ds(pl.multiple_of(dx * chans + lanes.start, strip), strip)
            ref[row, :, place] = part.astype(jnp.bfloat16)

    def scale_rows(count, place):
        @pl.loop(0, count * strips)
        def _(index):
            row, lanes = place(index // strips), lanes_of(index)
            value = raw[row, :, lanes].astype(jnp.float32) * gain_ref[0:1, lanes]
            put_shifted(sh, row, lanes, value)

    gain_ref[...] = jnp.broadcast_to(gain, gain_ref.shape)
    locals_[0].wait()
    scale_rows(rows, lambda r: r + rows)
    acc[...] = jnp.zeros_like(acc)
    acc2[...] = jnp.zeros_like(acc2)

    pl.semaphore_wait(barrier, members - 1 + bands - 1)

    if n2 > 1:
        u, v = 1 + core * (n1 - 1), n1 - core * (n1 - 1)
    else:
        u, v = 1, members
    p1 = lax.rem(me // u, n1)
    p2 = lax.rem(me // v, n2)

    def member_at(q1, q2):
        return q1 * u + q2 * v

    def back(i1, i2):
        return member_at(lax.rem(p1 - i1 + n1, n1), lax.rem(p2 - i2 + n2, n2))

    chunks = chunk_count(shard)

    def half(ref, base, which, chunk):
        if shard % (32 * chunks) == 0:
            size = shard // (2 * chunks)
            first = base + which * (shard // 2) + chunk * size
            return ref.at[pl.ds(pl.multiple_of(first, 16), size)]
        span = ref.shape[1] // 2
        return ref.at[
            pl.ds(pl.multiple_of(base, 16), shard), pl.ds(pl.multiple_of(which * span, 128), span)
        ]

    def leg_copy(w, i1, i2, chunk):
        src, buf = ((w1, wb1), (w2, wb2))[w]
        dest = member_at(lax.rem(p1 + i1, n1), lax.rem(p2 + i2, n2))
        return pltpu.make_async_remote_copy(
            src_ref=half(src, 0, core, chunk),
            dst_ref=half(buf, me * shard, core, chunk),
            send_sem=leg_send.at[w, i1, i2, chunk],
            recv_sem=leg_recv.at[w, i1, i2, chunk],
            device_id=(dest, lat),
            device_id_type=MESH,
        )

    def sib_copy(w, i1, i2, chunk):
        buf = (wb1, wb2)[w]
        place = half(buf, back(i1, i2) * shard, core, chunk)
        return pltpu.make_async_remote_copy(
            src_ref=place,
            dst_ref=place,
            send_sem=sib_send.at[w, i1, i2, chunk],
            recv_sem=sib_recv.at[w, i1, i2, chunk],
            device_id=(me, sibling),
            device_id_type=MESH,
        )

    def send_own(w, some):
        for chunk in some:
            for i1, i2 in offsets[1:]:
                leg_copy(w, i1, i2, chunk).start()

    def arrive(w, i1, i2, some=range(chunks)):
        for chunk in some:
            leg_copy(w, i1, i2, chunk).wait_recv()
            sib_copy(w, i1, i2, chunk).start()

    def halo_copy(step):
        place = pl.ds(0, rows) if step > 0 else pl.ds(2 * rows, rows)
        index = 0 if step > 0 else 1
        return pltpu.make_async_remote_copy(
            src_ref=states.at[0],
            dst_ref=raw.at[place],
            send_sem=halo_send.at[index],
            recv_sem=halo_recv.at[index],
            device_id=(me, lat + step),
            device_id_type=MESH,
        )

    send_own(0, range(chunks))
    has_low, has_high = lat > 0, lat < bands - 1

    @pl.when(has_high)
    def _():
        halo_copy(1).start()

    @pl.when(has_low)
    def _():
        halo_copy(-1).start()

    for chunk in range(chunks):
        for i1 in range(1, n1):
            arrive(0, i1, 0, [chunk])
        send_own(1, [chunk])


    @pl.when(has_low)
    def _():
        halo_copy(1).wait_recv()

    @pl.when(jnp.logical_not(has_low))
    def _():
        raw[0:rows] = jnp.zeros((rows, cols, chans), jnp.bfloat16)

    @pl.when(has_high)
    def _():
        halo_copy(-1).wait_recv()

    @pl.when(jnp.logical_not(has_high))
    def _():
        raw[2 * rows : 3 * rows] = jnp.zeros((rows, cols, chans), jnp.bfloat16)

    scale_rows(2 * rows, lambda r: r + rows * (r // rows))

    code = jnp.int32(0)
    combo = me * 2 + core
    for index, value in enumerate(codes):
        code = jnp.where(combo == index, jnp.int32(value), code)

    def stage_waits(w, stage):
        i1, i2 = offsets[stage]
        if stage == 0:
            locals_[1 + w].wait()
            return
        if legs(i1, i2) > legs(*offsets[stage - 1]):
            if w == 0 and legs(i1, i2) == 2:
                for o1 in range(1, n1):
                    arrive(1, o1, 0)
            for o1, o2 in offsets:
                if legs(o1, o2) == legs(i1, i2) and o2 > 0:
                    arrive(w, o1, o2)
        for chunk in range(chunks):
            sib_copy(w, *((i2, i1) if n2 > 1 else (i1, i2)), chunk).wait_recv()

    def conv(w, field, total, count, base):
        buf = (wb1, wb2)[w]

        def step(i, left_code):
            done = 0
            for at in range(ROWTAPS):
                due = list(range(done, stage_of[at] + 1))
                done = max(done, stage_of[at] + 1)
                if due:

                    @pl.when(i == at)
                    def _():
                        for stage in due:
                            stage_waits(w, stage)

            deep = ROWTAPS * chans
            dy = lax.rem(left_code, ROWTAPS)
            left = field[pl.ds(base + dy, count)].reshape(count * cols, deep)
            right = buf[pl.ds(pl.multiple_of(dy * deep, 128), deep), :]
            total[...] += jnp.dot(left, right, preferred_element_type=jnp.float32)
            return left_code // ROWTAPS

        lax.fori_loop(0, ROWTAPS, step, code)
        if w == 0 and n2 == 1:
            for o1 in range(1, n1):
                arrive(1, o1, 0)

    conv(0, sh, acc, rows + 2, rows - 2)
    @pl.loop(0, (rows + 2) * strips)
    def _(index):
        row, lanes = index // strips, lanes_of(index)
        at = pl.ds(pl.multiple_of(row * cols, cols), cols)
        value = jax.nn.gelu(acc[at, lanes], approximate=True)
        inside = jnp.logical_and(
            jnp.logical_or(row > 0, has_low), jnp.logical_or(row < rows + 1, has_high)
        )
        put_shifted(ish, row, lanes, jnp.where(inside, value, 0.0))

    conv(1, ish, acc2, rows, 0)

    own = sh[pl.ds(rows, rows), :, pl.ds(chans, chans)].reshape(rows * cols, chans).astype(jnp.float32)
    block = (own + acc2[...]).astype(jnp.bfloat16)
    pred = lax.dot_general(
        head[...], block, (((1,), (1,)), ((), ())), preferred_element_type=jnp.float32
    )
    pred = jnp.concatenate([pred[:, r * cols : (r + 1) * cols] for r in range(rows)], axis=0)
    preds[me] = pred.astype(jnp.bfloat16)

    pred_copies = [
        pltpu.make_async_remote_copy(
            src_ref=preds.at[me],
            dst_ref=preds.at[me],
            send_sem=pred_send.at[j],
            recv_sem=pred_recv.at[j],
            device_id=(lax.rem(me + j, members), lat),
            device_id_type=MESH,
        )
        for j in range(1, members)
    ]
    for copy in pred_copies:
        copy.start()
    for copy in pred_copies:
        copy.wait_recv()

    eps = 0.05 / members
    factor = (1.0 - eps) / (2.0 * members * (members - 1))
    truth = jnp.concatenate([target[:, r, :] for r in range(rows)], axis=0)
    all_preds = [preds[m].astype(jnp.float32) for m in range(members)]
    skill = sum(jnp.abs(p - truth) for p in all_preds) / members
    pairs = sum(
        jnp.abs(all_preds[m] - all_preds[n]) for m in range(members) for n in range(m)
    )
    score = skill - (2.0 * factor) * pairs
    weighted = jnp.zeros((fields, 128), jnp.float32)
    for r in range(rows):
        piece = score[r * fields : (r + 1) * fields]
        score_ref[:, r, :] = piece
        piece = sum(piece[:, c : c + 128] for c in range(0, cols, 128))
        weighted = weighted + piece * areas[r]
    parts[lat] = weighted

    part_copies = [
        pltpu.make_async_remote_copy(
            src_ref=parts.at[lat],
            dst_ref=parts.at[lat],
            send_sem=part_send.at[j],
            recv_sem=part_recv.at[j],
            device_id=(me, lax.rem(lat + j, bands)),
            device_id_type=MESH,
        )
        for j in range(1, bands)
    ]
    for copy in part_copies:
        copy.start()
    for copy in part_copies:
        copy.wait_recv()
    total = jnp.sum(parts[...], axis=0)
    total = jnp.sum(jnp.sum(total, axis=0, keepdims=True), axis=1, keepdims=True)
    mean = total / (fields * cols * area_total)
    mean_ref[0, 0] = mean[0, 0]

    @pl.when(has_high)
    def _():
        halo_copy(1).wait_send()

    @pl.when(has_low)
    def _():
        halo_copy(-1).wait_send()

    for w in range(2):
        for i1, i2 in offsets[1:]:
            for chunk in range(chunks):
                leg_copy(w, i1, i2, chunk).wait_send()
                sib_copy(w, i1, i2, chunk).wait_send()
    for copy in pred_copies + part_copies:
        copy.wait_send()


def body(members, bands, *args):
    states, head = args[0], args[5]
    rows, cols, chans = states.shape[1:]
    fields = head.shape[1]
    args = args[:5] + (head.T,) + args[6:]
    n1, n2 = route(members)
    chunks = chunk_count(args[3].shape[0])
    hbm = pl.BlockSpec(memory_space=pltpu.HBM)
    vmem = pl.BlockSpec(memory_space=pltpu.VMEM)
    smem = pl.BlockSpec(memory_space=pltpu.SMEM)
    dma = pltpu.SemaphoreType.DMA
    bf16, f32 = jnp.bfloat16, jnp.float32
    score, mean = pl.pallas_call(
        functools.partial(kernel, members, bands),
        out_shape=(
            jax.ShapeDtypeStruct((fields, rows, cols), f32),
            jax.ShapeDtypeStruct((1, 1), f32),
        ),
        in_specs=[hbm] * 8,
        out_specs=(vmem, smem),
        scratch_shapes=[
            pltpu.SMEM((1,), jnp.int32),
            pltpu.VMEM(args[2].shape, f32),
            pltpu.VMEM((fields, chans), bf16),
            pltpu.VMEM(args[6].shape, f32),
            pltpu.SMEM((1,), jnp.int32),
            pltpu.VMEM((8, chans), f32),
            pltpu.VMEM((3 * rows, cols, chans), bf16),
            pltpu.VMEM((3 * rows, cols, ROWTAPS * chans), bf16),
            pltpu.VMEM((rows + 2, cols, ROWTAPS * chans), bf16),
            pltpu.VMEM((TAPS * chans, chans), bf16),
            pltpu.VMEM((TAPS * chans, chans), bf16),
            pltpu.VMEM(((rows + 2) * cols, chans), f32),
            pltpu.VMEM((rows * cols, chans), f32),
            pltpu.VMEM((members, rows * fields, cols), bf16),
            pltpu.VMEM((bands, fields, 128), f32),
            dma((8,)),
            dma((2,)),
            dma((2,)),
            dma((2, n1, n2, chunks)),
            dma((2, n1, n2, chunks)),
            dma((2, n1, n2, chunks)),
            dma((2, n1, n2, chunks)),
            dma((members,)),
            dma((members,)),
            dma((bands,)),
            dma((bands,)),
        ],
        compiler_params=pltpu.CompilerParams(
            collective_id=0, has_side_effects=True, vmem_limit_bytes=62 * 1024 * 1024
        ),
        cost_estimate=pl.CostEstimate(
            flops=2 * 6 * cols * TAPS * chans * chans,
            bytes_accessed=4 * TAPS * chans * chans,
            transcendentals=4 * cols * chans,
        ),
    )(*args)
    return score, mean[0, 0]


def solution(mesh):
    placed = (
        P("member", "lat", None, None),
        P("member"),
        P(),
        P("member", None),
        P("member", None),
        P(),
        P(None, "lat", None),
        P(),
    )
    return jax.shard_map(
        functools.partial(body, mesh.shape["member"], mesh.shape["lat"]),
        mesh=mesh,
        in_specs=placed,
        out_specs=(P(None, "lat", None), P()),
        check_vma=False,
    )
```

```python
import functools
import math

import jax
import jax.numpy as jnp
import numpy as np
from jax import lax
from jax.experimental import pallas as pl
from jax.experimental.pallas import tpu as pltpu
from jax.sharding import PartitionSpec as P

MESH = pl.DeviceIdType.MESH
TAPS = 9
ROWTAPS = 3


def route(members):
    side = math.isqrt(members)
    return (side, side) if side * side == members else (members, 1)


def legs(i1, i2):
    return (i1 > 0) + (i2 > 0)


def tap_plan(members, chans):
    n1, n2 = route(members)
    shard = TAPS * chans // members
    offsets = sorted(
        ((i1, i2) for i1 in range(n1) for i2 in range(n2)), key=lambda o: legs(*o)
    )
    codes, stages = [], []
    for me in range(members):
        for core in range(2):
            u, v = (1 + core * (n1 - 1), n1 - core * (n1 - 1)) if n2 > 1 else (1, members)
            p1, p2 = (me // u) % n1, (me // v) % n2
            arrival = {}
            for stage, (i1, i2) in enumerate(offsets):
                arrival[((p1 - i1) % n1) * u + ((p2 - i2) % n2) * v] = stage
            deep = ROWTAPS * chans
            need = [
                max(arrival[s] for s in range(g * deep // shard, ((g + 1) * deep - 1) // shard + 1))
                for g in range(ROWTAPS)
            ]
            order = sorted(range(ROWTAPS), key=lambda g: need[g])
            codes.append(sum(g * ROWTAPS**i for i, g in enumerate(order)))
            stages.append([need[g] for g in order])
    return offsets, codes, np.max(np.array(stages), axis=0).tolist()


def chunk_count(shard):
    return 2 if shard % 64 == 0 else 1


def kernel(
    members, bands, states, ident_hbm, gains_hbm, w1, w2, head_hbm, target_hbm, first_row_hbm,
    score_ref, mean_ref, ident, gains, head, target, first_row, gain_ref, raw, sh, ish, wb1, wb2, acc, acc2, preds, parts,
    local_sem, halo_send, halo_recv, leg_send, leg_recv, sib_send, sib_recv,
    pred_send, pred_recv, part_send, part_recv,
):
    rows, cols, chans = states.shape[1:]
    fields = head_hbm.shape[0]
    shard = w1.shape[0]
    n1, n2 = route(members)
    offsets, codes, stage_of = tap_plan(members, chans)
    me = lax.axis_index("member")
    lat = lax.axis_index("lat")
    core = lax.rem(lat, 2)
    sibling = lat + 1 - 2 * core

    barrier = pltpu.get_barrier_semaphore()
    for j in range(1, members):
        pl.semaphore_signal(
            barrier, inc=1, device_id=(lax.rem(me + j, members), lat), device_id_type=MESH
        )
    for j in range(1, bands):
        pl.semaphore_signal(
            barrier, inc=1, device_id=(me, lax.rem(lat + j, bands)), device_id_type=MESH
        )

    own_rows = pl.ds(pl.multiple_of(me * shard, 16), shard)
    locals_ = [
        pltpu.make_async_copy(states.at[0], raw.at[pl.ds(rows, rows)], local_sem.at[0]),
        pltpu.make_async_copy(w1, wb1.at[own_rows], local_sem.at[1]),
        pltpu.make_async_copy(w2, wb2.at[own_rows], local_sem.at[2]),
    ]
    small = [
        pltpu.make_async_copy(source, place, local_sem.at[3 + index])
        for index, (source, place) in enumerate(
            (
                (ident_hbm, ident),
                (gains_hbm, gains),
                (first_row_hbm, first_row),
                (head_hbm, head),
                (target_hbm, target),
            )
        )
    ]
    for copy in small + locals_:
        copy.start()
    pl.semaphore_wait(barrier, members - 1 + bands - 1)

    if n2 > 1:
        u, v = 1 + core * (n1 - 1), n1 - core * (n1 - 1)
    else:
        u, v = 1, members
    p1 = lax.rem(me // u, n1)
    p2 = lax.rem(me // v, n2)

    def member_at(q1, q2):
        return q1 * u + q2 * v

    def back(i1, i2):
        return member_at(lax.rem(p1 - i1 + n1, n1), lax.rem(p2 - i2 + n2, n2))

    chunks = chunk_count(shard)

    def half(ref, base, which, chunk):
        if shard % (32 * chunks) == 0:
            size = shard // (2 * chunks)
            first = base + which * (shard // 2) + chunk * size
            return ref.at[pl.ds(pl.multiple_of(first, 16), size)]
        span = ref.shape[1] // 2
        return ref.at[
            pl.ds(pl.multiple_of(base, 16), shard), pl.ds(pl.multiple_of(which * span, 128), span)
        ]

    def leg_copy(w, i1, i2, chunk):
        src, buf = ((w1, wb1), (w2, wb2))[w]
        if i2 == 0:
            dest = member_at(lax.rem(p1 + i1, n1), p2)
            origin, j1 = me, 0
        else:
            dest = member_at(p1, lax.rem(p2 + i2, n2))
            origin, j1 = back(i1, 0), i1
        source = (
            half(src, 0, core, chunk) if j1 == 0 else half(buf, origin * shard, core, chunk)
        )
        return pltpu.make_async_remote_copy(
            src_ref=source,
            dst_ref=half(buf, origin * shard, core, chunk),
            send_sem=leg_send.at[w, i1, i2, chunk],
            recv_sem=leg_recv.at[w, i1, i2, chunk],
            device_id=(dest, lat),
            device_id_type=MESH,
        )

    def sib_copy(w, i1, i2, chunk):
        buf = (wb1, wb2)[w]
        place = half(buf, back(i1, i2) * shard, core, chunk)
        return pltpu.make_async_remote_copy(
            src_ref=place,
            dst_ref=place,
            send_sem=sib_send.at[w, i1, i2, chunk],
            recv_sem=sib_recv.at[w, i1, i2, chunk],
            device_id=(me, sibling),
            device_id_type=MESH,
        )

    def send_own(w, some):
        for chunk in some:
            for i1 in range(1, n1):
                leg_copy(w, i1, 0, chunk).start()
            for i2 in range(1, n2):
                leg_copy(w, 0, i2, chunk).start()

    def arrive(w, i1, i2, some=range(chunks)):
        for chunk in some:
            leg_copy(w, i1, i2, chunk).wait_recv()
            if i2 == 0:
                for j2 in range(1, n2):
                    leg_copy(w, i1, j2, chunk).start()
            sib_copy(w, i1, i2, chunk).start()

    def halo_copy(step):
        place = pl.ds(0, rows) if step > 0 else pl.ds(2 * rows, rows)
        index = 0 if step > 0 else 1
        return pltpu.make_async_remote_copy(
            src_ref=states.at[0],
            dst_ref=raw.at[place],
            send_sem=halo_send.at[index],
            recv_sem=halo_recv.at[index],
            device_id=(me, lat + step),
            device_id_type=MESH,
        )

    send_own(0, range(chunks))
    has_low, has_high = lat > 0, lat < bands - 1

    @pl.when(has_high)
    def _():
        halo_copy(1).start()

    @pl.when(has_low)
    def _():
        halo_copy(-1).start()

    for copy in small:
        copy.wait()

    lane = lax.broadcasted_iota(jnp.int32, gains.shape, 0)
    gain = jnp.sum(jnp.where(lane == ident[0], gains[...], 0.0), axis=0, keepdims=True)

    all_rows = rows * bands
    width = -(-all_rows // 128) * 128
    ids = lax.broadcasted_iota(jnp.int32, (8, width), 1)
    area_all = jnp.cos(jnp.pi * (90.0 - 0.1 * (first_row[0] + ids).astype(jnp.float32)) / 180.0)

    def area_sum(chosen):
        return jnp.sum(jnp.where(chosen, area_all, 0.0)[0:1], axis=1, keepdims=True)

    area_total = area_sum(ids < all_rows)
    areas = [area_sum(ids == lat * rows + r) for r in range(rows)]

    strip = 128
    strips = chans // strip
    place_ids = lax.broadcasted_iota(jnp.int32, (cols, strip), 0)

    def lanes_of(index):
        return pl.ds(pl.multiple_of(lax.rem(index, strips) * strip, strip), strip)

    def put_shifted(ref, row, lanes, value):
        low = jnp.where(place_ids == 0, 0.0, pltpu.roll(value, 1, 0))
        high = jnp.where(place_ids == cols - 1, 0.0, pltpu.roll(value, cols - 1, 0))
        for dx, part in enumerate((low, value, high)):
            place = pl.ds(pl.multiple_of(dx * chans + lanes.start, strip), strip)
            ref[row, :, place] = part.astype(jnp.bfloat16)

    def scale_rows(count, place):
        @pl.loop(0, count * strips)
        def _(index):
            row, lanes = place(index // strips), lanes_of(index)
            value = raw[row, :, lanes].astype(jnp.float32) * gain_ref[0:1, lanes]
            put_shifted(sh, row, lanes, value)

    gain_ref[...] = jnp.broadcast_to(gain, gain_ref.shape)
    locals_[0].wait()
    scale_rows(rows, lambda r: r + rows)

    for chunk in range(chunks):
        for i1 in range(1, n1):
            arrive(0, i1, 0, [chunk])
        send_own(1, [chunk])
    acc[...] = jnp.zeros_like(acc)
    acc2[...] = jnp.zeros_like(acc2)


    @pl.when(has_low)
    def _():
        halo_copy(1).wait_recv()

    @pl.when(jnp.logical_not(has_low))
    def _():
        raw[0:rows] = jnp.zeros((rows, cols, chans), jnp.bfloat16)

    @pl.when(has_high)
    def _():
        halo_copy(-1).wait_recv()

    @pl.when(jnp.logical_not(has_high))
    def _():
        raw[2 * rows : 3 * rows] = jnp.zeros((rows, cols, chans), jnp.bfloat16)

    scale_rows(2 * rows, lambda r: r + rows * (r // rows))

    code = jnp.int32(0)
    combo = me * 2 + core
    for index, value in enumerate(codes):
        code = jnp.where(combo == index, jnp.int32(value), code)

    def stage_waits(w, stage):
        i1, i2 = offsets[stage]
        if stage == 0:
            locals_[1 + w].wait()
            return
        if legs(i1, i2) > legs(*offsets[stage - 1]):
            if w == 0 and legs(i1, i2) == 2:
                for o1 in range(1, n1):
                    arrive(1, o1, 0)
            for o1, o2 in offsets:
                if legs(o1, o2) == legs(i1, i2) and o2 > 0:
                    arrive(w, o1, o2)
        for chunk in range(chunks):
            sib_copy(w, *((i2, i1) if n2 > 1 else (i1, i2)), chunk).wait_recv()

    def conv(w, field, total, count, base):
        buf = (wb1, wb2)[w]

        def step(i, left_code):
            done = 0
            for at in range(ROWTAPS):
                due = list(range(done, stage_of[at] + 1))
                done = max(done, stage_of[at] + 1)
                if due:

                    @pl.when(i == at)
                    def _():
                        for stage in due:
                            stage_waits(w, stage)

            deep = ROWTAPS * chans
            dy = lax.rem(left_code, ROWTAPS)
            left = field[pl.ds(base + dy, count)].reshape(count * cols, deep)
            right = buf[pl.ds(pl.multiple_of(dy * deep, 128), deep), :]
            total[...] += jnp.dot(left, right, preferred_element_type=jnp.float32)
            return left_code // ROWTAPS

        lax.fori_loop(0, ROWTAPS, step, code)
        if w == 0 and n2 == 1:
            for o1 in range(1, n1):
                arrive(1, o1, 0)

    conv(0, sh, acc, rows + 2, rows - 2)
    @pl.loop(0, (rows + 2) * strips)
    def _(index):
        row, lanes = index // strips, lanes_of(index)
        at = pl.ds(pl.multiple_of(row * cols, cols), cols)
        value = jax.nn.gelu(acc[at, lanes], approximate=True)
        inside = jnp.logical_and(
            jnp.logical_or(row > 0, has_low), jnp.logical_or(row < rows + 1, has_high)
        )
        put_shifted(ish, row, lanes, jnp.where(inside, value, 0.0))

    conv(1, ish, acc2, rows, 0)

    own = sh[pl.ds(rows, rows), :, pl.ds(chans, chans)].reshape(rows * cols, chans).astype(jnp.float32)
    block = (own + acc2[...]).astype(jnp.bfloat16)
    pred = lax.dot_general(
        head[...], block, (((1,), (1,)), ((), ())), preferred_element_type=jnp.float32
    )
    pred = jnp.concatenate([pred[:, r * cols : (r + 1) * cols] for r in range(rows)], axis=0)
    preds[me] = pred.astype(jnp.bfloat16)

    pred_copies = [
        pltpu.make_async_remote_copy(
            src_ref=preds.at[me],
            dst_ref=preds.at[me],
            send_sem=pred_send.at[j],
            recv_sem=pred_recv.at[j],
            device_id=(lax.rem(me + j, members), lat),
            device_id_type=MESH,
        )
        for j in range(1, members)
    ]
    for copy in pred_copies:
        copy.start()
    for copy in pred_copies:
        copy.wait_recv()

    eps = 0.05 / members
    factor = (1.0 - eps) / (2.0 * members * (members - 1))
    truth = jnp.concatenate([target[:, r, :] for r in range(rows)], axis=0)
    all_preds = [preds[m].astype(jnp.float32) for m in range(members)]
    skill = sum(jnp.abs(p - truth) for p in all_preds) / members
    pairs = sum(
        jnp.abs(all_preds[m] - all_preds[n]) for m in range(members) for n in range(m)
    )
    score = skill - (2.0 * factor) * pairs
    weighted = jnp.zeros((fields, 128), jnp.float32)
    for r in range(rows):
        piece = score[r * fields : (r + 1) * fields]
        score_ref[:, r, :] = piece
        piece = sum(piece[:, c : c + 128] for c in range(0, cols, 128))
        weighted = weighted + piece * areas[r]
    parts[lat] = weighted

    part_copies = [
        pltpu.make_async_remote_copy(
            src_ref=parts.at[lat],
            dst_ref=parts.at[lat],
            send_sem=part_send.at[j],
            recv_sem=part_recv.at[j],
            device_id=(me, lax.rem(lat + j, bands)),
            device_id_type=MESH,
        )
        for j in range(1, bands)
    ]
    for copy in part_copies:
        copy.start()
    for copy in part_copies:
        copy.wait_recv()
    total = jnp.sum(parts[...], axis=0)
    total = jnp.sum(jnp.sum(total, axis=0, keepdims=True), axis=1, keepdims=True)
    mean = total / (fields * cols * area_total)
    mean_ref[0, 0] = mean[0, 0]

    @pl.when(has_high)
    def _():
        halo_copy(1).wait_send()

    @pl.when(has_low)
    def _():
        halo_copy(-1).wait_send()

    for w in range(2):
        for i1, i2 in offsets[1:]:
            for chunk in range(chunks):
                leg_copy(w, i1, i2, chunk).wait_send()
                sib_copy(w, i1, i2, chunk).wait_send()
    for copy in pred_copies + part_copies:
        copy.wait_send()


def body(members, bands, *args):
    states, head = args[0], args[5]
    rows, cols, chans = states.shape[1:]
    fields = head.shape[1]
    args = args[:5] + (head.T,) + args[6:]
    n1, n2 = route(members)
    chunks = chunk_count(args[3].shape[0])
    hbm = pl.BlockSpec(memory_space=pltpu.HBM)
    vmem = pl.BlockSpec(memory_space=pltpu.VMEM)
    smem = pl.BlockSpec(memory_space=pltpu.SMEM)
    dma = pltpu.SemaphoreType.DMA
    bf16, f32 = jnp.bfloat16, jnp.float32
    score, mean = pl.pallas_call(
        functools.partial(kernel, members, bands),
        out_shape=(
            jax.ShapeDtypeStruct((fields, rows, cols), f32),
            jax.ShapeDtypeStruct((1, 1), f32),
        ),
        in_specs=[hbm] * 8,
        out_specs=(vmem, smem),
        scratch_shapes=[
            pltpu.SMEM((1,), jnp.int32),
            pltpu.VMEM(args[2].shape, f32),
            pltpu.VMEM((fields, chans), bf16),
            pltpu.VMEM(args[6].shape, f32),
            pltpu.SMEM((1,), jnp.int32),
            pltpu.VMEM((8, chans), f32),
            pltpu.VMEM((3 * rows, cols, chans), bf16),
            pltpu.VMEM((3 * rows, cols, ROWTAPS * chans), bf16),
            pltpu.VMEM((rows + 2, cols, ROWTAPS * chans), bf16),
            pltpu.VMEM((TAPS * chans, chans), bf16),
            pltpu.VMEM((TAPS * chans, chans), bf16),
            pltpu.VMEM(((rows + 2) * cols, chans), f32),
            pltpu.VMEM((rows * cols, chans), f32),
            pltpu.VMEM((members, rows * fields, cols), bf16),
            pltpu.VMEM((bands, fields, 128), f32),
            dma((8,)),
            dma((2,)),
            dma((2,)),
            dma((2, n1, n2, chunks)),
            dma((2, n1, n2, chunks)),
            dma((2, n1, n2, chunks)),
            dma((2, n1, n2, chunks)),
            dma((members,)),
            dma((members,)),
            dma((bands,)),
            dma((bands,)),
        ],
        compiler_params=pltpu.CompilerParams(
            collective_id=0, has_side_effects=True, vmem_limit_bytes=62 * 1024 * 1024
        ),
        cost_estimate=pl.CostEstimate(
            flops=2 * 6 * cols * TAPS * chans * chans,
            bytes_accessed=4 * TAPS * chans * chans,
            transcendentals=4 * cols * chans,
        ),
    )(*args)
    return score, mean[0, 0]


def solution(mesh):
    placed = (
        P("member", "lat", None, None),
        P("member"),
        P(),
        P("member", None),
        P("member", None),
        P(),
        P(None, "lat", None),
        P(),
    )
    return jax.shard_map(
        functools.partial(body, mesh.shape["member"], mesh.shape["lat"]),
        mesh=mesh,
        in_specs=placed,
        out_specs=(P(None, "lat", None), P()),
        check_vma=False,
    )
```

```python
import functools
import math

import jax
import jax.numpy as jnp
import numpy as np
from jax import lax
from jax.experimental import pallas as pl
from jax.experimental.pallas import tpu as pltpu
from jax.sharding import PartitionSpec as P

MESH = pl.DeviceIdType.MESH
TAPS = 9
ROWTAPS = 3


def route(members):
    side = math.isqrt(members)
    return (side, side) if side * side == members else (members, 1)


def legs(i1, i2):
    return (i1 > 0) + (i2 > 0)


def tap_plan(members, chans):
    n1, n2 = route(members)
    shard = TAPS * chans // members
    offsets = sorted(
        ((i1, i2) for i1 in range(n1) for i2 in range(n2)), key=lambda o: legs(*o)
    )
    codes, stages = [], []
    for me in range(members):
        for core in range(2):
            u, v = (1 + core * (n1 - 1), n1 - core * (n1 - 1)) if n2 > 1 else (1, members)
            p1, p2 = (me // u) % n1, (me // v) % n2
            arrival = {}
            for stage, (i1, i2) in enumerate(offsets):
                arrival[((p1 - i1) % n1) * u + ((p2 - i2) % n2) * v] = stage
            deep = ROWTAPS * chans
            need = [
                max(arrival[s] for s in range(g * deep // shard, ((g + 1) * deep - 1) // shard + 1))
                for g in range(ROWTAPS)
            ]
            order = sorted(range(ROWTAPS), key=lambda g: need[g])
            codes.append(sum(g * ROWTAPS**i for i, g in enumerate(order)))
            stages.append([need[g] for g in order])
    return offsets, codes, np.max(np.array(stages), axis=0).tolist()


def chunk_count(shard):
    return 2 if shard % 64 == 0 else 1


def kernel(
    members, bands, states, ident_hbm, gains_hbm, w1, w2, head_hbm, target_hbm, first_row_hbm,
    score_ref, mean_ref, ident, gains, head, target, first_row, gain_ref, raw, sh, ish, wb1, wb2, acc, acc2, preds, parts,
    local_sem, halo_send, halo_recv, leg_send, leg_recv, sib_send, sib_recv,
    pred_send, pred_recv, part_send, part_recv,
):
    rows, cols, chans = states.shape[1:]
    fields = head_hbm.shape[0]
    shard = w1.shape[0]
    n1, n2 = route(members)
    offsets, codes, stage_of = tap_plan(members, chans)
    me = lax.axis_index("member")
    lat = lax.axis_index("lat")
    core = lax.rem(lat, 2)
    sibling = lat + 1 - 2 * core

    barrier = pltpu.get_barrier_semaphore()
    for j in range(1, members):
        pl.semaphore_signal(
            barrier, inc=1, device_id=(lax.rem(me + j, members), lat), device_id_type=MESH
        )
    for j in range(1, bands):
        pl.semaphore_signal(
            barrier, inc=1, device_id=(me, lax.rem(lat + j, bands)), device_id_type=MESH
        )

    own_rows = pl.ds(pl.multiple_of(me * shard, 16), shard)
    locals_ = [
        pltpu.make_async_copy(states.at[0], raw.at[pl.ds(rows, rows)], local_sem.at[0]),
        pltpu.make_async_copy(w1, wb1.at[own_rows], local_sem.at[1]),
        pltpu.make_async_copy(w2, wb2.at[own_rows], local_sem.at[2]),
    ]
    small = [
        pltpu.make_async_copy(source, place, local_sem.at[3 + index])
        for index, (source, place) in enumerate(
            (
                (ident_hbm, ident),
                (gains_hbm, gains),
                (first_row_hbm, first_row),
                (head_hbm, head),
                (target_hbm, target),
            )
        )
    ]
    for copy in small + locals_:
        copy.start()
    pl.semaphore_wait(barrier, members - 1 + bands - 1)

    if n2 > 1:
        u, v = 1 + core * (n1 - 1), n1 - core * (n1 - 1)
    else:
        u, v = 1, members
    p1 = lax.rem(me // u, n1)
    p2 = lax.rem(me // v, n2)

    def member_at(q1, q2):
        return q1 * u + q2 * v

    def back(i1, i2):
        return member_at(lax.rem(p1 - i1 + n1, n1), lax.rem(p2 - i2 + n2, n2))

    chunks = chunk_count(shard)

    def half(ref, base, which, chunk):
        if shard % (32 * chunks) == 0:
            size = shard // (2 * chunks)
            first = base + which * (shard // 2) + chunk * size
            return ref.at[pl.ds(pl.multiple_of(first, 16), size)]
        span = ref.shape[1] // 2
        return ref.at[
            pl.ds(pl.multiple_of(base, 16), shard), pl.ds(pl.multiple_of(which * span, 128), span)
        ]

    def leg_copy(w, i1, i2, chunk):
        src, buf = ((w1, wb1), (w2, wb2))[w]
        if i2 == 0:
            dest = member_at(lax.rem(p1 + i1, n1), p2)
            origin, j1 = me, 0
        else:
            dest = member_at(p1, lax.rem(p2 + i2, n2))
            origin, j1 = back(i1, 0), i1
        source = (
            half(src, 0, core, chunk) if j1 == 0 else half(buf, origin * shard, core, chunk)
        )
        return pltpu.make_async_remote_copy(
            src_ref=source,
            dst_ref=half(buf, origin * shard, core, chunk),
            send_sem=leg_send.at[w, i1, i2, chunk],
            recv_sem=leg_recv.at[w, i1, i2, chunk],
            device_id=(dest, lat),
            device_id_type=MESH,
        )

    def sib_copy(w, i1, i2, chunk):
        buf = (wb1, wb2)[w]
        place = half(buf, back(i1, i2) * shard, core, chunk)
        return pltpu.make_async_remote_copy(
            src_ref=place,
            dst_ref=place,
            send_sem=sib_send.at[w, i1, i2, chunk],
            recv_sem=sib_recv.at[w, i1, i2, chunk],
            device_id=(me, sibling),
            device_id_type=MESH,
        )

    def send_own(w, some):
        for chunk in some:
            for i1 in range(1, n1):
                leg_copy(w, i1, 0, chunk).start()
            for i2 in range(1, n2):
                leg_copy(w, 0, i2, chunk).start()

    def arrive(w, i1, i2, some=range(chunks)):
        for chunk in some:
            leg_copy(w, i1, i2, chunk).wait_recv()
            if i2 == 0:
                for j2 in range(1, n2):
                    leg_copy(w, i1, j2, chunk).start()
            sib_copy(w, i1, i2, chunk).start()

    def halo_copy(step):
        place = pl.ds(0, rows) if step > 0 else pl.ds(2 * rows, rows)
        index = 0 if step > 0 else 1
        return pltpu.make_async_remote_copy(
            src_ref=states.at[0],
            dst_ref=raw.at[place],
            send_sem=halo_send.at[index],
            recv_sem=halo_recv.at[index],
            device_id=(me, lat + step),
            device_id_type=MESH,
        )

    send_own(0, range(chunks))
    has_low, has_high = lat > 0, lat < bands - 1

    @pl.when(has_high)
    def _():
        halo_copy(1).start()

    @pl.when(has_low)
    def _():
        halo_copy(-1).start()

    for copy in small:
        copy.wait()

    lane = lax.broadcasted_iota(jnp.int32, gains.shape, 0)
    gain = jnp.sum(jnp.where(lane == ident[0], gains[...], 0.0), axis=0, keepdims=True)

    all_rows = rows * bands
    width = -(-all_rows // 128) * 128
    ids = lax.broadcasted_iota(jnp.int32, (8, width), 1)
    area_all = jnp.cos(jnp.pi * (90.0 - 0.1 * (first_row[0] + ids).astype(jnp.float32)) / 180.0)

    def area_sum(chosen):
        return jnp.sum(jnp.where(chosen, area_all, 0.0)[0:1], axis=1, keepdims=True)

    area_total = area_sum(ids < all_rows)
    areas = [area_sum(ids == lat * rows + r) for r in range(rows)]

    strip = 128
    strips = chans // strip
    place_ids = lax.broadcasted_iota(jnp.int32, (cols, strip), 0)

    def lanes_of(index):
        return pl.ds(pl.multiple_of(lax.rem(index, strips) * strip, strip), strip)

    def put_shifted(ref, row, lanes, value):
        low = jnp.where(place_ids == 0, 0.0, pltpu.roll(value, 1, 0))
        high = jnp.where(place_ids == cols - 1, 0.0, pltpu.roll(value, cols - 1, 0))
        for dx, part in enumerate((low, value, high)):
            place = pl.ds(pl.multiple_of(dx * chans + lanes.start, strip), strip)
            ref[row, :, place] = part.astype(jnp.bfloat16)

    def scale_rows(count, place):
        @pl.loop(0, count * strips)
        def _(index):
            row, lanes = place(index // strips), lanes_of(index)
            value = raw[row, :, lanes].astype(jnp.float32) * gain_ref[0:1, lanes]
            put_shifted(sh, row, lanes, value)

    gain_ref[...] = jnp.broadcast_to(gain, gain_ref.shape)
    locals_[0].wait()
    scale_rows(rows, lambda r: r + rows)

    for chunk in range(chunks):
        for i1 in range(1, n1):
            arrive(0, i1, 0, [chunk])
        send_own(1, [chunk])
    acc[...] = jnp.zeros_like(acc)
    acc2[...] = jnp.zeros_like(acc2)


    @pl.when(has_low)
    def _():
        halo_copy(1).wait_recv()

    @pl.when(jnp.logical_not(has_low))
    def _():
        raw[0:rows] = jnp.zeros((rows, cols, chans), jnp.bfloat16)

    @pl.when(has_high)
    def _():
        halo_copy(-1).wait_recv()

    @pl.when(jnp.logical_not(has_high))
    def _():
        raw[2 * rows : 3 * rows] = jnp.zeros((rows, cols, chans), jnp.bfloat16)

    scale_rows(2 * rows, lambda r: r + rows * (r // rows))

    code = jnp.int32(0)
    combo = me * 2 + core
    for index, value in enumerate(codes):
        code = jnp.where(combo == index, jnp.int32(value), code)

    def stage_waits(w, stage):
        i1, i2 = offsets[stage]
        if stage == 0:
            locals_[1 + w].wait()
            return
        if legs(i1, i2) > legs(*offsets[stage - 1]):
            for o1, o2 in offsets:
                if legs(o1, o2) == legs(i1, i2) and o2 > 0:
                    arrive(w, o1, o2)
            if w == 0 and legs(i1, i2) == 2:
                for o1 in range(1, n1):
                    arrive(1, o1, 0)
        for chunk in range(chunks):
            sib_copy(w, *((i2, i1) if n2 > 1 else (i1, i2)), chunk).wait_recv()

    def conv(w, field, total, count, base):
        buf = (wb1, wb2)[w]

        def step(i, left_code):
            done = 0
            for at in range(ROWTAPS):
                due = list(range(done, stage_of[at] + 1))
                done = max(done, stage_of[at] + 1)
                if due:

                    @pl.when(i == at)
                    def _():
                        for stage in due:
                            stage_waits(w, stage)

            deep = ROWTAPS * chans
            dy = lax.rem(left_code, ROWTAPS)
            left = field[pl.ds(base + dy, count)].reshape(count * cols, deep)
            right = buf[pl.ds(pl.multiple_of(dy * deep, 128), deep), :]
            total[...] += jnp.dot(left, right, preferred_element_type=jnp.float32)
            return left_code // ROWTAPS

        lax.fori_loop(0, ROWTAPS, step, code)
        if w == 0 and n2 == 1:
            for o1 in range(1, n1):
                arrive(1, o1, 0)

    conv(0, sh, acc, rows + 2, rows - 2)
    @pl.loop(0, (rows + 2) * strips)
    def _(index):
        row, lanes = index // strips, lanes_of(index)
        at = pl.ds(pl.multiple_of(row * cols, cols), cols)
        value = jax.nn.gelu(acc[at, lanes], approximate=True)
        inside = jnp.logical_and(
            jnp.logical_or(row > 0, has_low), jnp.logical_or(row < rows + 1, has_high)
        )
        put_shifted(ish, row, lanes, jnp.where(inside, value, 0.0))

    conv(1, ish, acc2, rows, 0)

    own = sh[pl.ds(rows, rows), :, pl.ds(chans, chans)].reshape(rows * cols, chans).astype(jnp.float32)
    block = (own + acc2[...]).astype(jnp.bfloat16)
    pred = lax.dot_general(
        head[...], block, (((1,), (1,)), ((), ())), preferred_element_type=jnp.float32
    )
    pred = jnp.concatenate([pred[:, r * cols : (r + 1) * cols] for r in range(rows)], axis=0)
    preds[me] = pred.astype(jnp.bfloat16)

    pred_copies = [
        pltpu.make_async_remote_copy(
            src_ref=preds.at[me],
            dst_ref=preds.at[me],
            send_sem=pred_send.at[j],
            recv_sem=pred_recv.at[j],
            device_id=(lax.rem(me + j, members), lat),
            device_id_type=MESH,
        )
        for j in range(1, members)
    ]
    for copy in pred_copies:
        copy.start()
    for copy in pred_copies:
        copy.wait_recv()

    eps = 0.05 / members
    factor = (1.0 - eps) / (2.0 * members * (members - 1))
    truth = jnp.concatenate([target[:, r, :] for r in range(rows)], axis=0)
    all_preds = [preds[m].astype(jnp.float32) for m in range(members)]
    skill = sum(jnp.abs(p - truth) for p in all_preds) / members
    pairs = sum(
        jnp.abs(all_preds[m] - all_preds[n]) for m in range(members) for n in range(m)
    )
    score = skill - (2.0 * factor) * pairs
    weighted = jnp.zeros((fields, 128), jnp.float32)
    for r in range(rows):
        piece = score[r * fields : (r + 1) * fields]
        score_ref[:, r, :] = piece
        piece = sum(piece[:, c : c + 128] for c in range(0, cols, 128))
        weighted = weighted + piece * areas[r]
    parts[lat] = weighted

    part_copies = [
        pltpu.make_async_remote_copy(
            src_ref=parts.at[lat],
            dst_ref=parts.at[lat],
            send_sem=part_send.at[j],
            recv_sem=part_recv.at[j],
            device_id=(me, lax.rem(lat + j, bands)),
            device_id_type=MESH,
        )
        for j in range(1, bands)
    ]
    for copy in part_copies:
        copy.start()
    for copy in part_copies:
        copy.wait_recv()
    total = jnp.sum(parts[...], axis=0)
    total = jnp.sum(jnp.sum(total, axis=0, keepdims=True), axis=1, keepdims=True)
    mean = total / (fields * cols * area_total)
    mean_ref[0, 0] = mean[0, 0]

    @pl.when(has_high)
    def _():
        halo_copy(1).wait_send()

    @pl.when(has_low)
    def _():
        halo_copy(-1).wait_send()

    for w in range(2):
        for i1, i2 in offsets[1:]:
            for chunk in range(chunks):
                leg_copy(w, i1, i2, chunk).wait_send()
                sib_copy(w, i1, i2, chunk).wait_send()
    for copy in pred_copies + part_copies:
        copy.wait_send()


def body(members, bands, *args):
    states, head = args[0], args[5]
    rows, cols, chans = states.shape[1:]
    fields = head.shape[1]
    args = args[:5] + (head.T,) + args[6:]
    n1, n2 = route(members)
    chunks = chunk_count(args[3].shape[0])
    hbm = pl.BlockSpec(memory_space=pltpu.HBM)
    vmem = pl.BlockSpec(memory_space=pltpu.VMEM)
    smem = pl.BlockSpec(memory_space=pltpu.SMEM)
    dma = pltpu.SemaphoreType.DMA
    bf16, f32 = jnp.bfloat16, jnp.float32
    score, mean = pl.pallas_call(
        functools.partial(kernel, members, bands),
        out_shape=(
            jax.ShapeDtypeStruct((fields, rows, cols), f32),
            jax.ShapeDtypeStruct((1, 1), f32),
        ),
        in_specs=[hbm] * 8,
        out_specs=(vmem, smem),
        scratch_shapes=[
            pltpu.SMEM((1,), jnp.int32),
            pltpu.VMEM(args[2].shape, f32),
            pltpu.VMEM((fields, chans), bf16),
            pltpu.VMEM(args[6].shape, f32),
            pltpu.SMEM((1,), jnp.int32),
            pltpu.VMEM((8, chans), f32),
            pltpu.VMEM((3 * rows, cols, chans), bf16),
            pltpu.VMEM((3 * rows, cols, ROWTAPS * chans), bf16),
            pltpu.VMEM((rows + 2, cols, ROWTAPS * chans), bf16),
            pltpu.VMEM((TAPS * chans, chans), bf16),
            pltpu.VMEM((TAPS * chans, chans), bf16),
            pltpu.VMEM(((rows + 2) * cols, chans), f32),
            pltpu.VMEM((rows * cols, chans), f32),
            pltpu.VMEM((members, rows * fields, cols), bf16),
            pltpu.VMEM((bands, fields, 128), f32),
            dma((8,)),
            dma((2,)),
            dma((2,)),
            dma((2, n1, n2, chunks)),
            dma((2, n1, n2, chunks)),
            dma((2, n1, n2, chunks)),
            dma((2, n1, n2, chunks)),
            dma((members,)),
            dma((members,)),
            dma((bands,)),
            dma((bands,)),
        ],
        compiler_params=pltpu.CompilerParams(
            collective_id=0, has_side_effects=True, vmem_limit_bytes=62 * 1024 * 1024
        ),
        cost_estimate=pl.CostEstimate(
            flops=2 * 6 * cols * TAPS * chans * chans,
            bytes_accessed=4 * TAPS * chans * chans,
            transcendentals=4 * cols * chans,
        ),
    )(*args)
    return score, mean[0, 0]


def solution(mesh):
    placed = (
        P("member", "lat", None, None),
        P("member"),
        P(),
        P("member", None),
        P("member", None),
        P(),
        P(None, "lat", None),
        P(),
    )
    return jax.shard_map(
        functools.partial(body, mesh.shape["member"], mesh.shape["lat"]),
        mesh=mesh,
        in_specs=placed,
        out_specs=(P(None, "lat", None), P()),
        check_vma=False,
    )
```
